256 devices in a mesh: tm: 8 (over y, x_hi), inner: 32 (over x_lo, z, core).
Axes of the slice: x: 4 (x_hi: 2, x_lo: 2; x = x_hi * 2 + x_lo), y: 4, z: 8, core: 2. Of those that a mesh axis runs over, the one named last changes fastest.
Arguments:
- frames: bfloat16 [256, 256, 768], P(('tm', 'inner')), may hold values from -6 to 6
- norm_gain: float32 [768], replicated, may hold values from 0.25 to 1.75
- w_qkv: bfloat16 [768, 2304], replicated, may hold values from -16 to 16
- w_out: bfloat16 [768, 768], replicated, may hold values from -0.21875 to 0.21875
- cotangent: bfloat16 [256, 256, 768], P(('tm', 'inner')), may hold values from -24 to 24
Outputs:
- block_out: bfloat16 [256, 256, 768], P(('tm', 'inner'))
- frames_grad: bfloat16 [256, 256, 768], P(('tm', 'inner'))
- qkv_weight_grad: float32 [768, 2304], P('inner', 'tm')
- out_weight_grad: float32 [768, 768], P('inner', 'tm')
- gain_grad: float32 [768], P('inner')
The draws below stay inside these ranges and needn't reach their ends.
All inputs are finite; a program needn't handle non-finite values.
Results may differ from the reference program's by a relative error of at most 0.012.
The reference program's roundings to bfloat16 on the way (of `normed`, `qkv_rows`, `weights_b`, `mixed_rows`, `grad_mix`, `score_grad` and `qkv_rows_grad`) count: a program that leaves them out, or rounds other values in their place, can miss the bound.
Values may be sent and summed in bfloat16 or wider, within the bound.
A program may use at most 128 MiB of HBM per device.

```python
import math
import jax
import jax.numpy as jnp
from jax import lax

D = 768
HEADS = 12
HEAD_DIM = 64
P_SIZE = 256
WINDOW = 4
FRAMES = 256
CLIP = 256
TOKENS = 65536


def draw_frames(key, part):
    key_one = jax.random.fold_in(key, 0)
    values = jax.random.normal(key_one, (FRAMES, P_SIZE, D), jnp.float32)
    return jnp.clip(values, -6.0, 6.0).astype(jnp.bfloat16)


def draw_w_qkv(key, part):
    key_one = jax.random.fold_in(key, 0)
    base_w = jnp.clip(jax.random.normal(key_one, (D, 3 * D), jnp.float32), -6.0, 6.0) / math.sqrt(D)
    return jnp.clip(base_w, -16.0, 16.0).astype(jnp.bfloat16)


def strengthened(array, rng, source, target, blocks, factor):
    def block_of(axis_at):
        return (jnp.arange(array.shape[axis_at]) // (array.shape[axis_at] // blocks)).reshape((-1,) + (1,) * (array.ndim - 1 - axis_at))

    first = jax.random.permutation(rng, blocks)[block_of(target)]
    other_side = (block_of(target) + blocks // 2) % blocks
    return jnp.where((block_of(source) == first) | (block_of(source) == other_side), factor * array, array)


def level_of(stream_key, extent, pieces, least, top_value):
    def one(dim, shards_of):
        heights = jax.random.uniform(jax.random.fold_in(jax.random.fold_in(stream_key, 6), dim), (shards_of,), jnp.float32, least / len(pieces), top_value / len(pieces))
        return jnp.repeat(jnp.exp(heights), extent[dim] // shards_of).reshape((-1,) + (1,) * (len(extent) - dim - 1))

    level = one(*pieces[0])
    for cut in pieces[1:]:
        level = level * one(*cut)
    return level


def scatter_about(rng, dims, scale, bound, shards=(), held_as=jnp.bfloat16):
    entries = jax.random.normal(rng, dims, jnp.float32) * scale
    if len(shards) > 0:
        entries = level_of(rng, dims, shards, -0.22, 0.18) * entries
    return jnp.clip(entries, min=-bound, max=bound).astype(held_as)


def noise_with(own_key, extent, scale, bound, shards, heavy, held_as=jnp.bfloat16):
    drawn = scale * jax.random.normal(own_key, extent, jnp.float32)
    if shards:
        drawn = drawn * level_of(own_key, extent, shards, -0.22, 0.18)
    return jnp.clip(strengthened(drawn, jax.random.fold_in(own_key, 3), *heavy), -bound, bound).astype(held_as)


def setup_inputs(seed: int = 0) -> dict:
    key_of = jax.random.split(jax.random.key(seed), 6)
    frames = draw_frames(jax.random.fold_in(key_of[5], 71), 0)
    norm_gain = jnp.clip(1.0 + 0.15 * jax.random.normal(key_of[1], (D,), jnp.float32), 0.25, 1.75)
    w_qkv = draw_w_qkv(jax.random.fold_in(key_of[5], 71), 0)
    w_out = scatter_about(key_of[3], (D, D), D ** -0.5, 0.21875)
    cotangent = noise_with(key_of[4], (FRAMES, P_SIZE, D), 1.0, 24.0, ((0, 256),), (0, 2, 256, 6.0))
    return dict(frames=frames, norm_gain=norm_gain, w_qkv=w_qkv, w_out=w_out, cotangent=cotangent)


EPSILON = 1e-06

def normalize(row_data, norm_gain):
    wide_vals = row_data.astype(jnp.float32)
    center = wide_vals - lax.optimization_barrier(jnp.mean(wide_vals, axis=-1, keepdims=True))
    spread = lax.rsqrt(lax.optimization_barrier(jnp.mean(center * center, axis=-1, keepdims=True)) + EPSILON)
    unit_rows = center * spread
    return ((unit_rows * norm_gain).astype(jnp.bfloat16), unit_rows, spread)

def norm_back(normed_grad, unit_rows, spread, norm_gain):
    scaled = normed_grad * norm_gain
    mean_one = lax.optimization_barrier(jnp.mean(scaled, axis=-1, keepdims=True))
    second = lax.optimization_barrier(jnp.mean(scaled * unit_rows, axis=-1, keepdims=True))
    return spread * (scaled - mean_one - unit_rows * second)

def project(row_data, weight):
    flat_rows = row_data.reshape(-1, row_data.shape[-1])
    result = jnp.dot(flat_rows, weight, preferred_element_type=jnp.float32)
    return result.reshape(row_data.shape[:-1] + (weight.shape[1],))

def project_back(row_data, weight):
    flat_rows = row_data.reshape(-1, row_data.shape[-1])
    result = lax.dot_general(flat_rows, weight, (((1,), (1,)), ((), ())), preferred_element_type=jnp.float32)
    return result.reshape(row_data.shape[:-1] + (weight.shape[0],))

def contract(left_rows, right_rows):
    left_flat = left_rows.reshape(-1, left_rows.shape[-1])
    right_flat = right_rows.reshape(-1, right_rows.shape[-1])
    return lax.dot_general(left_flat, right_flat, (((0,), (0,)), ((), ())), preferred_element_type=jnp.float32)

def heads_of(row_data):
    return row_data.reshape(row_data.shape[:-1] + (HEADS, HEAD_DIM))

def attend(query_rows, key_pad, value_pad, first_frame, all_frames, clip_len):
    held_frames = query_rows.shape[0]
    span_len = 2 * WINDOW + 1
    score_scale = HEAD_DIM ** (-0.5)
    query_h = heads_of(query_rows).astype(jnp.float32)
    score_list = []
    for offset in range(span_len):
        key_h = heads_of(key_pad[offset:offset + held_frames]).astype(jnp.float32)
        score_list.append(jnp.einsum('ftnd,ftnd->ftn', query_h, key_h))
    scores = jnp.stack(score_list) * score_scale
    query_at = first_frame + jnp.arange(held_frames)[None, :]
    frame_at = query_at + jnp.arange(span_len)[:, None] - WINDOW
    inside = (frame_at >= 0) & (frame_at < all_frames) & (frame_at // clip_len == query_at // clip_len)
    inside = inside[:, :, None, None]
    scores = jnp.where(inside, scores, -1e+30)
    row_top = lax.optimization_barrier(jnp.max(scores, axis=0, keepdims=True))
    exp_scores = jnp.exp(scores - row_top)
    soft_probs = exp_scores / lax.optimization_barrier(jnp.sum(exp_scores, axis=0, keepdims=True))
    weights_b = soft_probs.astype(jnp.bfloat16)
    mixed_rows = jnp.zeros(query_h.shape, jnp.float32)
    for offset in range(span_len):
        value_h = heads_of(value_pad[offset:offset + held_frames]).astype(jnp.float32)
        mixed_rows = mixed_rows + weights_b[offset][..., None].astype(jnp.float32) * value_h
    mixed_rows = mixed_rows.reshape(query_rows.shape).astype(jnp.bfloat16)
    return (mixed_rows, soft_probs, weights_b)

def attend_back(query_rows, key_pad, value_pad, soft_probs, weights_b, grad_mix):
    held_frames = query_rows.shape[0]
    span_len = 2 * WINDOW + 1
    score_scale = HEAD_DIM ** (-0.5)
    query_h = heads_of(query_rows).astype(jnp.float32)
    grad_h = heads_of(grad_mix).astype(jnp.float32)
    dot_list = []
    for offset in range(span_len):
        value_h = heads_of(value_pad[offset:offset + held_frames]).astype(jnp.float32)
        dot_list.append(jnp.einsum('ftnd,ftnd->ftn', grad_h, value_h))
    grad_dots = jnp.stack(dot_list)
    centre = lax.optimization_barrier(jnp.sum(soft_probs * grad_dots, axis=0, keepdims=True))
    score_grad = (soft_probs * (grad_dots - centre) * score_scale).astype(jnp.bfloat16)
    pad_shape = (key_pad.shape[0],) + query_h.shape[1:]
    query_grad = jnp.zeros(query_h.shape, jnp.float32)
    key_grad = jnp.zeros(pad_shape, jnp.float32)
    value_grad = jnp.zeros(pad_shape, jnp.float32)
    for offset in range(span_len):
        key_h = heads_of(key_pad[offset:offset + held_frames]).astype(jnp.float32)
        score_w = score_grad[offset][..., None].astype(jnp.float32)
        query_grad = query_grad + score_w * key_h
        key_grad = key_grad.at[offset:offset + held_frames].add(score_w * query_h)
        value_grad = value_grad.at[offset:offset + held_frames].add(weights_b[offset][..., None].astype(jnp.float32) * grad_h)
    flat_shape = (key_pad.shape[0],) + query_rows.shape[1:]
    pad_grad = jnp.concatenate([key_grad.reshape(flat_shape), value_grad.reshape(flat_shape)], -1)
    return (query_grad.reshape(query_rows.shape), pad_grad)

def reference(frames, norm_gain, w_qkv, w_out, cotangent):
    feat_width = D
    normed, unit_rows, spread = normalize(frames, norm_gain)
    qkv_rows = project(normed, w_qkv).astype(jnp.bfloat16)
    kv_pad = jnp.pad(qkv_rows[..., feat_width:], ((WINDOW, WINDOW), (0, 0), (0, 0)))
    query_rows = qkv_rows[..., :feat_width]
    mixed_rows, soft_probs, weights_b = attend(query_rows, kv_pad[..., :feat_width], kv_pad[..., feat_width:], 0, FRAMES, CLIP)
    block_out = (frames.astype(jnp.float32) + project(mixed_rows, w_out)).astype(jnp.bfloat16)
    out_grad = contract(mixed_rows, cotangent)
    grad_mix = project_back(cotangent, w_out).astype(jnp.bfloat16)
    query_grad, pad_grad = attend_back(query_rows, kv_pad[..., :feat_width], kv_pad[..., feat_width:], soft_probs, weights_b, grad_mix)
    kv_grad = pad_grad[WINDOW:WINDOW + FRAMES]
    qkv_rows_grad = jnp.concatenate([query_grad, kv_grad], -1).astype(jnp.bfloat16)
    qkv_grad = contract(normed, qkv_rows_grad)
    normed_grad = project_back(qkv_rows_grad, w_qkv)
    gain_part = lax.optimization_barrier(jnp.sum(normed_grad * unit_rows, axis=(0, 1)))
    frames_grad = (cotangent.astype(jnp.float32) + norm_back(normed_grad, unit_rows, spread, norm_gain)).astype(jnp.bfloat16)
    inv_root = 1.0 / math.sqrt(TOKENS)
    return (block_out, frames_grad, qkv_grad * inv_root, out_grad * inv_root, gain_part * inv_root)
```

```python
import functools
import math

import jax
import jax.numpy as jnp
from jax import lax
from jax.experimental import pallas as pl
from jax.experimental.pallas import tpu as pltpu
from jax.sharding import PartitionSpec as P

HEAD_DIM = 64
WINDOW = 4
CLIP_MAX = 256
EPSILON = 1e-06
SPAN = 2 * WINDOW + 1
WIDE = 128
CORES = 2
X_LO = 2
X_HI = 2
MESH = pl.DeviceIdType.MESH
F32 = jnp.float32
BF16 = jnp.bfloat16


def dot(a, b, dims=((1,), (0,))):
    return lax.dot_general(a, b, (dims, ((), ())), preferred_element_type=F32)


def split(wide_vals):
    high = wide_vals.astype(BF16)
    low = (wide_vals - high.astype(F32)).astype(BF16)
    return jnp.concatenate([high, low], axis=1)


def attention_kernel(
    sizes,
    x_ref,
    gain_ref,
    wqkv_ref,
    wout_ref,
    cot_ref,
    bo_ref,
    fg_ref,
    nrm_ref,
    mix_ref,
    dqkv_ref,
    gg_ref,
    halo,
    comp,
    rcomp,
    wd,
    unit,
    spread,
    ones,
    pick,
    spill,
    send_sem,
    recv_sem,
    csend_sem,
    crecv_sem,
):
    frames_all, inner, clip = sizes
    tokens, width = x_ref.shape
    chunks = width // WIDE
    rows_tile = 64
    f = lax.axis_index("tm") * inner + lax.axis_index("inner")
    odd = lax.rem(f, 2)

    def at(offset):
        g = lax.rem(f + offset + frames_all, frames_all)
        return (lax.div(g, inner), lax.rem(g, inner))

    others = [j for j in range(-WINDOW, WINDOW + 1) if j != 0]
    barrier = pltpu.get_barrier_semaphore()
    for j in others:
        pl.semaphore_signal(barrier, inc=1, device_id=at(j), device_id_type=MESH)

    wide_vals = x_ref[...].astype(F32)
    center = wide_vals - jnp.mean(wide_vals, axis=-1, keepdims=True)
    spread_one = lax.rsqrt(jnp.mean(center * center, axis=-1, keepdims=True) + EPSILON)
    unit_rows = center * spread_one
    unit[...] = unit_rows
    spread[...] = spread_one
    nrm_ref[...] = (unit_rows * gain_ref[...]).astype(BF16)

    row_at = lax.broadcasted_iota(jnp.int32, (2 * WIDE, WIDE), 0)
    lane_at = lax.broadcasted_iota(jnp.int32, (2 * WIDE, WIDE), 1)
    same = (lax.rem(row_at, WIDE) // HEAD_DIM) == (lane_at // HEAD_DIM)
    ones[...] = jnp.where(same, 1.0, 0.0).astype(BF16)
    row_at = lax.broadcasted_iota(jnp.int32, (16, 2 * WIDE), 0)
    lane_at = lax.broadcasted_iota(jnp.int32, (16, 2 * WIDE), 1)
    pick[...] = jnp.where(lane_at == row_at * HEAD_DIM, 1.0, 0.0).astype(BF16)
    spill[...] = jnp.where(lane_at // HEAD_DIM == row_at, 1.0, 0.0).astype(BF16)

    pl.semaphore_wait(barrier, len(others))

    def copy(c, k):
        if k < 4:
            source = (4, 4, 2, 6)[k]
            target = (2, 6, 0, 8)[k]
            where = at((2, -2, 2, -2)[k])
        else:
            source = (4, 2, 6, 8 - 8 * odd)[k - 4]
            target = source - 1 + 2 * odd
            where = at(1 - 2 * odd)
        return pltpu.make_async_remote_copy(
            src_ref=halo.at[c, source],
            dst_ref=halo.at[c, target],
            send_sem=send_sem.at[c, k],
            recv_sem=recv_sem.at[c, k],
            device_id=where,
            device_id_type=MESH,
        )

    def comp_copy(c, j):
        k = j + WINDOW
        return pltpu.make_async_remote_copy(
            src_ref=comp.at[c, k],
            dst_ref=rcomp.at[c, SPAN - 1 - k],
            send_sem=csend_sem.at[c, k],
            recv_sem=crecv_sem.at[c, k],
            device_id=at(j),
            device_id_type=MESH,
        )

    def columns(c, part):
        return pl.ds(pl.multiple_of(part * width + c * WIDE, WIDE), WIDE)

    def project(c):
        for part in range(3):
            result = dot(nrm_ref[...], wqkv_ref[:, columns(c, part)])
            halo[c, 4, :, part * WIDE : (part + 1) * WIDE] = result.astype(BF16)
        rows = pl.ds(pl.multiple_of(c * WIDE, WIDE), WIDE)
        result = dot(cot_ref[...], wout_ref[rows, :], ((1,), (1,)))
        halo[c, 4, :, 3 * WIDE : 4 * WIDE] = result.astype(BF16)
        for k in (0, 1, 4):
            copy(c, k).start()

    def relay(c):
        copy(c, 0).wait_recv()
        copy(c, 2).start()
        copy(c, 5).start()
        copy(c, 1).wait_recv()
        copy(c, 3).start()
        copy(c, 6).start()

    def relay_last(c):
        copy(c, 2).wait_recv()
        copy(c, 3).wait_recv()
        copy(c, 7).start()

    def attend(c):
        for k in (4, 5, 6, 7):
            copy(c, k).wait_recv()

        @pl.loop(0, tokens // rows_tile)
        def _(i):
            rows = pl.ds(pl.multiple_of(i * rows_tile, rows_tile), rows_tile)
            query = halo[c, 4, rows, 0:WIDE].astype(F32)
            grad = halo[c, 4, rows, 3 * WIDE : 4 * WIDE].astype(F32)
            products = []
            for k in range(SPAN):
                products.append(split(query * halo[c, k, rows, WIDE : 2 * WIDE].astype(F32)))
            scores = dot(jnp.concatenate(products, axis=0), ones[...]) * (HEAD_DIM**-0.5)
            products = []
            for k in range(SPAN):
                products.append(
                    split(grad * halo[c, k, rows, 2 * WIDE : 3 * WIDE].astype(F32))
                )
            dots = dot(jnp.concatenate(products, axis=0), ones[...])
            score = []
            for k in range(SPAN):
                g = f + (k - WINDOW)
                inside = (g >= 0) & (g < frames_all)
                inside = inside & (lax.div(g + clip, clip) == lax.div(f + clip, clip))
                cap = jnp.where(inside, 3e38, -1e30).astype(F32)
                score.append(jnp.minimum(scores[k * rows_tile : (k + 1) * rows_tile], cap))
            top = functools.reduce(jnp.maximum, score)
            raised = [jnp.exp(s - top) for s in score]
            scale = 1.0 / functools.reduce(jnp.add, raised)
            soft = [e * scale for e in raised]
            mixed = jnp.zeros((rows_tile, WIDE), F32)
            centre = jnp.zeros((rows_tile, WIDE), F32)
            for k in range(SPAN):
                weight = soft[k].astype(BF16)
                wd[k, rows, 0:WIDE] = weight
                mixed += weight.astype(F32) * halo[c, k, rows, 2 * WIDE : 3 * WIDE].astype(F32)
                centre += soft[k] * dots[k * rows_tile : (k + 1) * rows_tile]
            mix_ref[rows, columns(c, 0)] = mixed.astype(BF16)
            query_grad = jnp.zeros((rows_tile, WIDE), F32)
            for k in range(SPAN):
                gap = dots[k * rows_tile : (k + 1) * rows_tile] - centre
                slope = (soft[k] * gap * (HEAD_DIM**-0.5)).astype(BF16)
                wd[k, rows, WIDE : 2 * WIDE] = slope
                query_grad += slope.astype(F32) * halo[c, k, rows, WIDE : 2 * WIDE].astype(F32)
            dqkv_ref[rows, columns(c, 0)] = query_grad.astype(BF16)

        for k in range(SPAN):
            small = dot(pick[...], wd[k], ((1,), (1,))).astype(BF16)
            if k == WINDOW:
                rcomp[c, k] = small
            else:
                comp[c, k] = small
                comp_copy(c, k - WINDOW).start()

    def collect(c):
        for j in others:
            comp_copy(c, j).wait_recv()
        half = 128
        for i in range(tokens // half):
            rows = slice(i * half, (i + 1) * half)
            key_grad = jnp.zeros((half, WIDE), F32)
            value_grad = jnp.zeros((half, WIDE), F32)
            for k in range(SPAN):
                wide = dot(rcomp[c, k, :, rows], spill[...], ((0,), (0,)))
                value_grad += wide[:, :WIDE] * halo[c, k, rows, 3 * WIDE : 4 * WIDE].astype(F32)
                key_grad += wide[:, WIDE:] * halo[c, k, rows, 0:WIDE].astype(F32)
            dqkv_ref[rows, columns(c, 1)] = key_grad.astype(BF16)
            dqkv_ref[rows, columns(c, 2)] = value_grad.astype(BF16)

    ahead = min(3, chunks)

    @pl.loop(0, ahead)
    def _(c):
        project(c)

    relay(0)

    @pl.loop(0, chunks + 1)
    def _(c):
        @pl.when(c + ahead < chunks)
        def _():
            project(c + ahead)

        @pl.when(c + 1 < chunks)
        def _():
            relay(c + 1)

        @pl.when(c < chunks)
        def _():
            relay_last(c)
            attend(c)

        @pl.when(c == chunks)
        def _():
            mixed_out = dot(mix_ref[...], wout_ref[...])
            bo_ref[...] = (x_ref[...].astype(F32) + mixed_out).astype(BF16)

        @pl.when(c > 0)
        def _():
            collect(c - 1)

    normed_grad = dot(dqkv_ref[...], wqkv_ref[...], ((1,), (1,)))
    unit_rows = unit[...]
    gain_part = jnp.sum(normed_grad * unit_rows, axis=0, keepdims=True)
    gg_ref[...] = jnp.zeros(gg_ref.shape, F32)
    for i in range(chunks):
        gg_ref[i : i + 1, :] = gain_part[:, i * WIDE : (i + 1) * WIDE]
    scaled = normed_grad * gain_ref[...]
    mean_one = jnp.mean(scaled, axis=-1, keepdims=True)
    second = jnp.mean(scaled * unit_rows, axis=-1, keepdims=True)
    back = spread[...] * (scaled - mean_one - unit_rows * second)
    fg_ref[...] = (cot_ref[...].astype(F32) + back).astype(BF16)

    @pl.loop(0, chunks)
    def _(c):
        for k in range(8):
            copy(c, k).wait_send()
        for j in others:
            comp_copy(c, j).wait_send()


def attention(mesh_sizes, x, gain, w_qkv, w_out, cot):
    tm_size, inner = mesh_sizes
    tokens, width = x.shape
    chunks = width // WIDE
    frames_all = tm_size * inner
    vmem = pl.BlockSpec(memory_space=pltpu.VMEM)
    sizes = (frames_all, inner, min(CLIP_MAX, frames_all))
    return pl.pallas_call(
        functools.partial(attention_kernel, sizes),
        out_shape=(
            jax.ShapeDtypeStruct((tokens, width), BF16),
            jax.ShapeDtypeStruct((tokens, width), BF16),
            jax.ShapeDtypeStruct((tokens, width), BF16),
            jax.ShapeDtypeStruct((tokens, width), BF16),
            jax.ShapeDtypeStruct((tokens, 3 * width), BF16),
            jax.ShapeDtypeStruct((8, WIDE), F32),
        ),
        in_specs=[vmem] * 5,
        out_specs=(vmem,) * 6,
        scratch_shapes=[
            pltpu.VMEM((chunks, SPAN, tokens, 4 * WIDE), BF16),
            pltpu.VMEM((chunks, SPAN, 16, tokens), BF16),
            pltpu.VMEM((chunks, SPAN, 16, tokens), BF16),
            pltpu.VMEM((SPAN, tokens, 2 * WIDE), BF16),
            pltpu.VMEM((tokens, width), F32),
            pltpu.VMEM((tokens, 1), F32),
            pltpu.VMEM((2 * WIDE, WIDE), BF16),
            pltpu.VMEM((16, 2 * WIDE), BF16),
            pltpu.VMEM((16, 2 * WIDE), BF16),
            pltpu.SemaphoreType.DMA((chunks, 8)),
            pltpu.SemaphoreType.DMA((chunks, 8)),
            pltpu.SemaphoreType.DMA((chunks, SPAN)),
            pltpu.SemaphoreType.DMA((chunks, SPAN)),
        ],
        compiler_params=pltpu.CompilerParams(
            collective_id=0, has_side_effects=True, vmem_limit_bytes=56 * 2**20
        ),
        name="windowed_attention",
    )(x, gain, w_qkv, w_out, cot)


def reduce_kernel(
    sizes,
    nrm_ref,
    mix_ref,
    right_ref,
    gain_ref,
    out_ref,
    gout_ref,
    core_send,
    core_recv,
    total,
    first_send,
    first_recv,
    next_total,
    next_send,
    next_recv,
    z_total,
    z_send,
    z_recv,
    final_send,
    final_recv,
    gain_core,
    gain_y,
    gain_x,
    gain_z,
    core_ssem,
    core_rsem,
    first_ssem,
    first_rsem,
    next_ssem,
    next_rsem,
    z_ssem,
    z_rsem,
    final_ssem,
    final_rsem,
    gain_ssem,
    gain_rsem,
):
    ny, nx, nz, left_width, inv_root = sizes
    halves = CORES
    rows = total.shape[1]
    part = rows // 2
    z_half = nz // halves
    z_rows = rows // z_half
    blocks = ny * nx
    tm_at = lax.axis_index("tm")
    inner_at = lax.axis_index("inner")
    core = lax.rem(inner_at, CORES)
    z = lax.rem(lax.div(inner_at, CORES), nz)
    x = lax.rem(tm_at, X_HI) * X_LO + lax.div(inner_at, CORES * nz)
    y = lax.div(tm_at, X_HI)

    def device(yy, xx, zz, cc):
        return (
            yy * X_HI + lax.div(xx, X_LO),
            (lax.rem(xx, X_LO) * nz + zz) * CORES + cc,
        )

    def turned(value, step, count):
        return lax.rem(value + step, count)

    peers = [device(y, x, z, 1 - core)]
    peers += [device(turned(y, d, ny), x, z, core) for d in range(1, ny)]
    peers += [device(y, turned(x, d, nx), z, core) for d in range(1, nx)]
    peers += [device(y, x, turned(z, d, nz), core) for d in range(1, nz)]
    barrier = pltpu.get_barrier_semaphore()
    for peer in peers:
        pl.semaphore_signal(barrier, inc=1, device_id=peer, device_id_type=MESH)
    pl.semaphore_wait(barrier, len(peers))

    def remote(source, target, ssem, rsem, where):
        return pltpu.make_async_remote_copy(
            src_ref=source,
            dst_ref=target,
            send_sem=ssem,
            recv_sem=rsem,
            device_id=where,
            device_id_type=MESH,
        )

    def gain_exchange(buffer, own, count, spot, slot):
        moves = []
        for d in range(1, count):
            moves.append(
                remote(
                    buffer.at[own],
                    buffer.at[own],
                    gain_ssem.at[slot, d],
                    gain_rsem.at[slot, d],
                    spot(turned(own, d, count)),
                )
            )
        return moves

    def gain_sum(buffer, count):
        value = buffer[0]
        for i in range(1, count):
            value = value + buffer[i]
        return value

    def weight_block(b, half):
        yy, xx = lax.div(b, nx), lax.rem(b, nx)
        t = yy * X_HI + lax.div(xx, X_LO)
        lo = lax.rem(xx, X_LO)
        right = right_ref[t]
        first = dot(nrm_ref[lo, half], right)
        second = dot(mix_ref[lo, half], right)
        lane = lax.broadcasted_iota(jnp.int32, first.shape, 1)
        return jnp.where(lane < left_width, first, second)

    def core_copy(b):
        return remote(
            core_send.at[b],
            core_recv.at[b],
            core_ssem.at[b],
            core_rsem.at[b],
            device(y, x, z, 1 - core),
        )

    gain_core[core] = gain_ref[...]
    core_gain = gain_exchange(
        gain_core, core, CORES, lambda cc: device(y, x, z, cc), 0
    )
    for move in core_gain:
        move.start()

    @pl.loop(0, blocks)
    def _(b):
        core_send[b] = weight_block(b, 1 - core).astype(BF16)
        core_copy(b).start()

    def first_copy(side, yy, xx):
        if side == 0:
            own, goal, line = y, yy, xx
            where = device(yy, x, z, core)
        else:
            own, goal, line = x, xx, yy
            where = device(y, xx, z, core)
        return remote(
            first_send.at[side, goal, line],
            first_recv.at[side, own, line],
            first_ssem.at[side, goal, line],
            first_rsem.at[side, own, line],
            where,
        )

    @pl.loop(0, blocks)
    def _(b):
        yy, xx = lax.div(b, nx), lax.rem(b, nx)
        own = weight_block(b, core)
        core_copy(b).wait_recv()
        own = own + core_recv[b].astype(F32)
        total[b] = own
        first_send[0, yy, xx] = own[:part].astype(BF16)
        first_send[1, xx, yy] = own[part:].astype(BF16)

        @pl.when(yy != y)
        def _():
            first_copy(0, yy, xx).start()

        @pl.when(xx != x)
        def _():
            first_copy(1, yy, xx).start()

    for move in core_gain:
        move.wait_recv()
    gain_y[y] = gain_sum(gain_core, CORES)
    y_gain = gain_exchange(gain_y, y, ny, lambda yy: device(yy, x, z, core), 1)
    for move in y_gain:
        move.start()

    def first_wait(side, d, line):
        own, count = (y, ny) if side == 0 else (x, nx)
        sender = turned(own, d, count)
        return sender, remote(
            first_send.at[side, sender, line],
            first_recv.at[side, sender, line],
            first_ssem.at[side, sender, line],
            first_rsem.at[side, sender, line],
            device(y, x, z, 1 - core),
        )

    def next_copy(side, d):
        if side == 0:
            own, goal = x, turned(x, d, nx)
            where = device(y, goal, z, core)
        else:
            own, goal = y, turned(y, d, ny)
            where = device(goal, x, z, core)
        return remote(
            next_send.at[side, goal],
            next_recv.at[side, own],
            next_ssem.at[side, d],
            next_rsem.at[side, d],
            where,
        )

    for side in range(2):
        count, lines = (ny, nx) if side == 0 else (nx, ny)
        own_line = x if side == 0 else y
        for step in range(1, lines + 1):
            line = turned(own_line, step, lines)
            b = y * nx + line if side == 0 else line * nx + x
            value = total[b, side * part : (side + 1) * part, :]
            for d in range(1, count):
                sender, move = first_wait(side, d, line)
                move.wait_recv()
                value = value + first_recv[side, sender, line].astype(F32)
            if step < lines:
                next_send[side, line] = value.astype(BF16)
                next_copy(side, step).start()
            else:
                next_total[side] = value

    for move in y_gain:
        move.wait_recv()
    gain_x[x] = gain_sum(gain_y, ny)
    x_gain = gain_exchange(gain_x, x, nx, lambda xx: device(y, xx, z, core), 2)
    for move in x_gain:
        move.start()

    def z_copy(goal):
        return remote(
            z_send.at[goal],
            z_recv.at[z],
            z_ssem.at[goal],
            z_rsem.at[z],
            device(y, x, core * z_half + goal, core),
        )

    for side in range(2):
        lines = nx if side == 0 else ny
        value = next_total[side]
        for d in range(1, lines):
            sender = turned(x if side == 0 else y, lines - d, lines)
            next_copy(side, d).wait_recv()
            value = value + next_recv[side, sender].astype(F32)
        for i in range(z_half // 2):
            goal = side * (z_half // 2) + i
            piece = value[i * z_rows : (i + 1) * z_rows]
            z_total[goal] = piece
            z_send[goal] = piece.astype(BF16)

            @pl.when(core * z_half + goal != z)
            def _():
                z_copy(goal).start()

    for move in x_gain:
        move.wait_recv()
    gain_z[z] = gain_sum(gain_x, nx)
    z_gain = gain_exchange(gain_z, z, nz, lambda zz: device(y, x, zz, core), 3)
    for move in z_gain:
        move.start()

    final = remote(
        final_send, final_recv, final_ssem, final_rsem, device(y, x, z, 1 - core)
    )
    owner = lax.div(z, z_half) == core
    final_rows = z_rows // CORES

    @pl.when(owner)
    def _():
        value = z_total[lax.rem(z, z_half)]
        for d in range(1, nz):
            sender = turned(z, d, nz)
            move = remote(
                z_send.at[0],
                z_recv.at[sender],
                z_ssem.at[0],
                z_rsem.at[sender],
                device(y, x, z, 1 - core),
            )
            move.wait_recv()
            value = value + z_recv[sender].astype(F32)
        value = value * inv_root
        lower = value[:final_rows]
        upper = value[final_rows:]
        mine = jnp.where(core == 0, lower, upper)
        final_send[...] = jnp.where(core == 0, upper, lower)
        final.start()
        out_ref[...] = mine
        final.wait_send()

    @pl.when(jnp.logical_not(owner))
    def _():
        final.wait_recv()
        out_ref[...] = final_recv[...]

    for move in z_gain:
        move.wait_recv()
    gout_ref[...] = gain_sum(gain_z, nz) * inv_root

    for move in core_gain + y_gain + x_gain + z_gain:
        move.wait_send()

    @pl.loop(0, blocks)
    def _(b):
        yy, xx = lax.div(b, nx), lax.rem(b, nx)
        core_copy(b).wait_send()

        @pl.when(yy != y)
        def _():
            first_copy(0, yy, xx).wait_send()

        @pl.when(xx != x)
        def _():
            first_copy(1, yy, xx).wait_send()

    for side in range(2):
        for d in range(1, nx if side == 0 else ny):
            next_copy(side, d).wait_send()
    for goal in range(z_half):

        @pl.when(core * z_half + goal != z)
        def _():
            z_copy(goal).wait_send()


def reduce_weights(mesh_sizes, normed, mixed, dqkv, cot, gain_part, inv_root):
    tm_size, inner = mesh_sizes
    tokens, width = normed.shape
    ny, nx = tm_size // X_HI, X_HI * X_LO
    nz = inner // (X_LO * CORES)
    left_width = 3 * width // tm_size
    block = 4 * width // tm_size
    rows = width // (X_LO * CORES)
    right = jnp.concatenate(
        [dqkv.reshape(tokens, tm_size, -1), cot.reshape(tokens, tm_size, -1)], axis=-1
    ).transpose(1, 0, 2)

    def cut(array):
        return array.T.reshape(X_LO, CORES, rows, tokens)

    part = rows // 2
    z_half = nz // CORES
    z_rows = rows // z_half
    final_rows = z_rows // CORES
    blocks = ny * nx
    most = max(nx, ny)
    vmem = pl.BlockSpec(memory_space=pltpu.VMEM)
    sizes = (ny, nx, nz, left_width, inv_root)
    dma = pltpu.SemaphoreType.DMA
    return pl.pallas_call(
        functools.partial(reduce_kernel, sizes),
        out_shape=(
            jax.ShapeDtypeStruct((final_rows, block), F32),
            jax.ShapeDtypeStruct((8, WIDE), F32),
        ),
        in_specs=[vmem] * 4,
        out_specs=(vmem,) * 2,
        scratch_shapes=[
            pltpu.VMEM((blocks, rows, block), BF16),
            pltpu.VMEM((blocks, rows, block), BF16),
            pltpu.VMEM((blocks, rows, block), F32),
            pltpu.VMEM((2, most, most, part, block), BF16),
            pltpu.VMEM((2, most, most, part, block), BF16),
            pltpu.VMEM((2, part, block), F32),
            pltpu.VMEM((2, most, part, block), BF16),
            pltpu.VMEM((2, most, part, block), BF16),
            pltpu.VMEM((z_half, z_rows, block), F32),
            pltpu.VMEM((z_half, z_rows, block), BF16),
            pltpu.VMEM((nz, z_rows, block), BF16),
            pltpu.VMEM((final_rows, block), F32),
            pltpu.VMEM((final_rows, block), F32),
            pltpu.VMEM((CORES, 8, WIDE), F32),
            pltpu.VMEM((ny, 8, WIDE), F32),
            pltpu.VMEM((nx, 8, WIDE), F32),
            pltpu.VMEM((nz, 8, WIDE), F32),
            dma((blocks,)),
            dma((blocks,)),
            dma((2, most, most)),
            dma((2, most, most)),
            dma((2, most)),
            dma((2, most)),
            dma((z_half,)),
            dma((nz,)),
            dma,
            dma,
            dma((4, nz)),
            dma((4, nz)),
        ],
        compiler_params=pltpu.CompilerParams(
            collective_id=1, has_side_effects=True, vmem_limit_bytes=48 * 2**20
        ),
        name="weight_reduction",
    )(cut(normed), cut(mixed), right, gain_part)


def shards(frames, norm_gain, w_qkv, w_out, cotangent):
    mesh_sizes = (lax.axis_size("tm"), lax.axis_size("inner"))
    tm_size, inner = mesh_sizes
    width = frames.shape[-1]
    tokens = frames.shape[0] * frames.shape[1]
    tokens_all = tokens * tm_size * inner
    x = frames.reshape(tokens, width)
    cot = cotangent.reshape(tokens, width)
    block_out, frames_grad, normed, mixed, dqkv, gain_part = attention(
        mesh_sizes, x, norm_gain.reshape(1, width), w_qkv, w_out, cot
    )
    inv_root = 1.0 / math.sqrt(tokens_all)
    weights, gain_sum = reduce_weights(
        mesh_sizes, normed, mixed, dqkv, cot, gain_part, inv_root
    )
    cut = 3 * width // tm_size
    share = width // inner
    gain_share = lax.dynamic_slice_in_dim(
        gain_sum.reshape(-1), lax.axis_index("inner") * share, share
    )
    return (
        block_out.reshape(frames.shape),
        frames_grad.reshape(frames.shape),
        weights[:, :cut],
        weights[:, cut:],
        gain_share,
    )


def solution(mesh):
    in_specs = (P(("tm", "inner"), None, None), P(), P(), P(), P(("tm", "inner"), None, None))
    out_specs = (
        P(("tm", "inner"), None, None),
        P(("tm", "inner"), None, None),
        P("inner", "tm"),
        P("inner", "tm"),
        P("inner"),
    )
    return jax.shard_map(shards, mesh=mesh, in_specs=in_specs, out_specs=out_specs, check_vma=False)
```

```python
import functools
import math

import jax
import jax.numpy as jnp
from jax import lax
from jax.experimental import pallas as pl
from jax.experimental.pallas import tpu as pltpu
from jax.sharding import PartitionSpec as P

HEAD_DIM = 64
WINDOW = 4
CLIP_MAX = 256
EPSILON = 1e-06
SPAN = 2 * WINDOW + 1
WIDE = 128
ROWS = 64
CORES = 2
X_LO = 2
X_HI = 2
MESH = pl.DeviceIdType.MESH
F32 = jnp.float32
BF16 = jnp.bfloat16


def dot(a, b, dims=((1,), (0,))):
    return lax.dot_general(a, b, (dims, ((), ())), preferred_element_type=F32)


def split(wide_vals):
    high = wide_vals.astype(BF16)
    low = (wide_vals - high.astype(F32)).astype(BF16)
    return jnp.concatenate([high, low], axis=1)


def remote(source, target, ssem, rsem, where):
    return pltpu.make_async_remote_copy(
        src_ref=source,
        dst_ref=target,
        send_sem=ssem,
        recv_sem=rsem,
        device_id=where,
        device_id_type=MESH,
    )


def turned(value, step, count):
    return lax.rem(value + step, count)


def block_kernel(
    sizes,
    x_ref,
    gain_ref,
    cot_ref,
    wqkv_hbm,
    wout_hbm,
    bo_ref,
    fg_ref,
    wq_ref,
    wo_ref,
    gout_ref,
    wqkv_ref,
    wout_ref,
    xn,
    halo,
    comp,
    rcomp,
    wd,
    stack,
    dqkv_ref,
    unit,
    spread,
    ones,
    pick,
    spill,
    right_own,
    right_other,
    nleft_own,
    nleft_other,
    mleft_own,
    mleft_other,
    left_t,
    total,
    f0_send,
    f0_recv,
    f1_send,
    f1_recv,
    n_total,
    n0_send,
    n0_recv,
    n1_send,
    n1_recv,
    z_total,
    z_send,
    z_recv,
    final_send,
    final_recv,
    gain_core,
    gain_y,
    gain_x,
    gain_z,
    load_sem,
    send_sem,
    recv_sem,
    csend_sem,
    crecv_sem,
    gsend_sem,
    grecv_sem,
    f0_ssem,
    f0_rsem,
    f1_ssem,
    f1_rsem,
    n0_ssem,
    n0_rsem,
    n1_ssem,
    n1_rsem,
    z_ssem,
    z_rsem,
    final_ssem,
    final_rsem,
    gain_ssem,
    gain_rsem,
):
    tm_size, inner, clip, inv_root = sizes
    frames_all = tm_size * inner
    tokens, width = x_ref.shape
    pairs = width // WIDE
    parts = tokens // ROWS
    ny, nx = tm_size // X_HI, X_HI * X_LO
    nz = inner // (X_LO * CORES)
    half_width = width // CORES
    share = 3 * width // tm_size
    block = 4 * width // tm_size
    side_rows = half_width // 2
    z_rows = half_width // nz
    final_rows = z_rows // CORES

    tm_at = lax.axis_index("tm")
    inner_at = lax.axis_index("inner")
    f = tm_at * inner + inner_at
    odd = lax.rem(f, 2)
    core = lax.rem(inner_at, CORES)
    z = lax.rem(lax.div(inner_at, CORES), nz)
    x_lo = lax.div(inner_at, CORES * nz)
    x_hi = lax.rem(tm_at, X_HI)
    x = x_hi * X_LO + x_lo
    y = lax.div(tm_at, X_HI)
    active = x_lo == core

    def at(offset):
        g = lax.rem(f + offset + frames_all, frames_all)
        return (lax.div(g, inner), lax.rem(g, inner))

    def device(yy, xx, zz, cc):
        return (
            yy * X_HI + lax.div(xx, X_LO),
            (lax.rem(xx, X_LO) * nz + zz) * CORES + cc,
        )

    partner = device(y, x, z, 1 - core)
    others = [j for j in range(-WINDOW, WINDOW + 1) if j != 0]
    peers = [at(j) for j in others]
    peers += [device(turned(y, d, ny), x, z, core) for d in range(1, ny)]
    peers += [device(y, turned(x, d, nx), z, core) for d in range(1, nx)]
    peers += [device(y, x, turned(z, d, nz), core) for d in range(1, nz)]
    barrier = pltpu.get_barrier_semaphore()
    for peer in peers:
        pl.semaphore_signal(barrier, inc=1, device_id=peer, device_id_type=MESH)

    load_qkv = pltpu.make_async_copy(wqkv_hbm, wqkv_ref, load_sem.at[0])
    load_out = pltpu.make_async_copy(wout_hbm, wout_ref, load_sem.at[1])
    load_qkv.start()
    load_out.start()

    wide_vals = x_ref[...].astype(F32)
    center = wide_vals - jnp.mean(wide_vals, axis=-1, keepdims=True)
    spread_one = lax.rsqrt(jnp.mean(center * center, axis=-1, keepdims=True) + EPSILON)
    unit_rows = center * spread_one
    unit[...] = unit_rows
    spread[...] = spread_one
    normed = (unit_rows * gain_ref[...]).astype(BF16)
    for p in range(parts):
        rows = slice(p * ROWS, (p + 1) * ROWS)
        xn[2, p, :, 0:width] = normed[rows]
        xn[2, p, :, width : 2 * width] = cot_ref[rows, :]
    for i in range(CORES):
        nleft_own[i] = normed[:, i * half_width : (i + 1) * half_width]

    def columns(c, part, size=WIDE):
        return pl.ds(pl.multiple_of(part * width + c * size, size), size)

    def copy(p, k):
        if k < 4:
            source = xn.at[(2, 2, 1, 3)[k], p]
            target = xn.at[(1, 3, 0, 4)[k], p]
            where = at((2, -2, 2, -2)[k])
        else:
            slot = (4, 2, 6, 8 - 8 * odd)[k - 4]
            source = halo.at[p, slot]
            target = halo.at[p, slot - 1 + 2 * odd]
            where = partner
        return remote(source, target, send_sem.at[p, k], recv_sem.at[p, k], where)

    def comp_copy(p, j):
        k = j + WINDOW
        return remote(
            comp.at[p, k],
            rcomp.at[p, SPAN - 1 - k],
            csend_sem.at[p, k],
            crecv_sem.at[p, k],
            at(j),
        )

    normed_copy = remote(
        nleft_own.at[1 - core], nleft_other, gsend_sem.at[0, 2], grecv_sem.at[0, 2], partner
    )

    def left_copy(p):
        return remote(
            mleft_own.at[1 - core, p],
            mleft_other.at[p],
            gsend_sem.at[p, 0],
            grecv_sem.at[p, 0],
            partner,
        )

    def right_copy(p):
        return remote(
            right_own.at[p], right_other.at[p], gsend_sem.at[p, 1], grecv_sem.at[p, 1], partner
        )

    pl.semaphore_wait(barrier, len(peers))

    @pl.loop(0, min(2, parts))
    def _(p):
        copy(p, 0).start()
        copy(p, 1).start()

    normed_copy.start()

    row_at = lax.broadcasted_iota(jnp.int32, (2 * WIDE, WIDE), 0)
    lane_at = lax.broadcasted_iota(jnp.int32, (2 * WIDE, WIDE), 1)
    same = (lax.rem(row_at, WIDE) // HEAD_DIM) == (lane_at // HEAD_DIM)
    ones[...] = jnp.where(same, 1.0, 0.0).astype(BF16)
    row_at = lax.broadcasted_iota(jnp.int32, pick.shape, 0)
    lane_at = lax.broadcasted_iota(jnp.int32, pick.shape, 1)
    pick[...] = jnp.where(row_at == lane_at * HEAD_DIM, 1.0, 0.0).astype(BF16)
    row_at = lax.broadcasted_iota(jnp.int32, spill.shape, 0)
    lane_at = lax.broadcasted_iota(jnp.int32, spill.shape, 1)
    spill[...] = jnp.where(lane_at // HEAD_DIM == row_at, 1.0, 0.0).astype(BF16)

    def place(p, value, start, stride, lead):
        left = value.shape[1]
        taken = 0
        while taken < left:
            t = (start + taken) // stride
            into = start + taken - t * stride
            count = min(left - taken, stride - into)
            right_own[p, t, :, lead + into : lead + into + count] = value[:, taken : taken + count]
            taken += count

    for p in range(parts):
        for m in range(pairs):
            value = cot_ref[p * ROWS : (p + 1) * ROWS, m * WIDE : (m + 1) * WIDE]
            place(p, value, m * WIDE, width // tm_size, share)

    load_qkv.wait()
    load_out.wait()

    def project(rows_in, put):
        for part in range(3):
            weight = wqkv_ref[:, part * width : (part + 1) * width]
            put(part, dot(rows_in[:, 0:width], weight).astype(BF16))
        put(3, dot(rows_in[:, width : 2 * width], wout_ref[...], ((1,), (1,))).astype(BF16))

    def put_own(part, value):
        for p in range(parts):
            halo[p, 4, :, part * width : (part + 1) * width] = value[p * ROWS : (p + 1) * ROWS]

    project(xn[2].reshape(tokens, 2 * width), put_own)

    @pl.loop(0, parts)
    def _(p):
        copy(p, 4).start()

    def relay(p):
        copy(p, 0).wait_recv()
        copy(p, 2).start()
        copy(p, 1).wait_recv()
        copy(p, 3).start()

    def project_others(p):
        copy(p, 2).wait_recv()
        copy(p, 3).wait_recv()
        rows_in = jnp.concatenate([xn[1, p], xn[3, p], xn[0, p], xn[4, p]], axis=0)

        def put(part, value):
            for i, k in enumerate((2, 6, 0, 8)):
                halo[p, k, :, part * width : (part + 1) * width] = value[
                    i * ROWS : (i + 1) * ROWS
                ]

        project(rows_in, put)
        for k in (5, 6, 7):
            copy(p, k).start()

    def attend(p):
        for k in (4, 5, 6, 7):
            copy(p, k).wait_recv()
        rows = pl.ds(pl.multiple_of(p * ROWS, ROWS), ROWS)

        @pl.loop(0, pairs)
        def _(c):
            def load(k, part):
                return halo[p, k, :, columns(c, part)].astype(F32)

            query = load(4, 0)
            grad = load(4, 3)
            products = [split(query * load(k, 1)) for k in range(SPAN)]
            scores = dot(jnp.concatenate(products, axis=0), ones[...]) * (HEAD_DIM**-0.5)
            products = [split(grad * load(k, 2)) for k in range(SPAN)]
            dots = dot(jnp.concatenate(products, axis=0), ones[...])
            score = []
            for k in range(SPAN):
                g = f + (k - WINDOW)
                inside = (g >= 0) & (g < frames_all)
                inside = inside & (lax.div(g + clip, clip) == lax.div(f + clip, clip))
                cap = jnp.where(inside, 3e38, -1e30).astype(F32)
                score.append(jnp.minimum(scores[k * ROWS : (k + 1) * ROWS], cap))
            top = functools.reduce(jnp.maximum, score)
            raised = [jnp.exp(s - top) for s in score]
            scale = 1.0 / functools.reduce(jnp.add, raised)
            soft = [e * scale for e in raised]
            mixed = jnp.zeros((ROWS, WIDE), F32)
            centre = jnp.zeros((ROWS, WIDE), F32)
            weight_at = pl.ds(pl.multiple_of(c * 2 * WIDE, WIDE), WIDE)
            slope_at = pl.ds(pl.multiple_of(c * 2 * WIDE + WIDE, WIDE), WIDE)
            for k in range(SPAN):
                weight = soft[k].astype(BF16)
                wd[k, :, weight_at] = weight
                mixed += weight.astype(F32) * load(k, 2)
                centre += soft[k] * dots[k * ROWS : (k + 1) * ROWS]
            side = lax.div(c, pairs // CORES)
            mleft_own[side, p, :, columns(lax.rem(c, pairs // CORES), 0)] = mixed.astype(BF16)
            query_grad = jnp.zeros((ROWS, WIDE), F32)
            for k in range(SPAN):
                gap = dots[k * ROWS : (k + 1) * ROWS] - centre
                slope = (soft[k] * gap * (HEAD_DIM**-0.5)).astype(BF16)
                wd[k, :, slope_at] = slope
                query_grad += slope.astype(F32) * load(k, 1)
            dqkv_ref[rows, columns(c, 0)] = query_grad.astype(BF16)

        small = dot(wd[...].reshape(SPAN * ROWS, 2 * width), pick[...])
        for k in range(SPAN):
            packed = small[k * ROWS : k * ROWS + 16]
            for r in range(1, ROWS // 16):
                at_row = k * ROWS + r * 16
                packed += pltpu.roll(small[at_row : at_row + 16], 32 * r, 1)
            if k == WINDOW:
                rcomp[p, k] = packed.astype(BF16)
            else:
                comp[p, k] = packed.astype(BF16)
                comp_copy(p, k - WINDOW).start()

    def collect(p):
        for j in others:
            comp_copy(p, j).wait_recv()
        rows = pl.ds(pl.multiple_of(p * ROWS, ROWS), ROWS)
        for k in range(SPAN):
            packed = rcomp[p, k].astype(F32)
            for r in range(ROWS // 16):
                value = packed if r == 0 else pltpu.roll(packed, WIDE - 32 * r, 1)
                stack[k * ROWS + r * 16 : k * ROWS + (r + 1) * 16, :] = value.astype(BF16)

        @pl.loop(0, pairs)
        def _(c):
            wide = dot(stack[...], spill[:, columns(c, 0, 2 * WIDE)])
            key_grad = jnp.zeros((ROWS, WIDE), F32)
            value_grad = jnp.zeros((ROWS, WIDE), F32)
            for k in range(SPAN):
                piece = wide[k * ROWS : (k + 1) * ROWS]
                value_grad += piece[:, :WIDE] * halo[p, k, :, columns(c, 3)].astype(F32)
                key_grad += piece[:, WIDE:] * halo[p, k, :, columns(c, 0)].astype(F32)
            dqkv_ref[rows, columns(c, 1)] = key_grad.astype(BF16)
            dqkv_ref[rows, columns(c, 2)] = value_grad.astype(BF16)

        for m in range(3 * pairs):
            value = dqkv_ref[rows, m * WIDE : (m + 1) * WIDE]
            place(p, value, m * WIDE, share, 0)
        left_copy(p).start()
        right_copy(p).start()

    relay(0)

    @pl.when(parts > 2)
    def _():
        copy(2, 0).start()
        copy(2, 1).start()

    if parts > 1:
        relay(1)
    project_others(0)

    @pl.loop(0, parts)
    def _(p):
        @pl.when(p + 3 < parts)
        def _():
            copy(p + 3, 0).start()
            copy(p + 3, 1).start()

        @pl.when(p + 2 < parts)
        def _():
            relay(p + 2)

        attend(p)

        @pl.when(p + 1 < parts)
        def _():
            project_others(p + 1)

        collect(p)

    def f0_copy(yy, xh):
        return remote(
            f0_send.at[yy, xh],
            f0_recv.at[y, xh],
            f0_ssem.at[yy, xh],
            f0_rsem.at[y, xh],
            device(yy, x, z, core),
        )

    def f1_copy(yy, xh):
        return remote(
            f1_send.at[xh, yy],
            f1_recv.at[x, yy],
            f1_ssem.at[xh, yy],
            f1_rsem.at[x, yy],
            device(y, xh * X_LO + core, z, core),
        )

    normed_copy.wait_recv()
    left_t[0, :, 0:tokens] = nleft_own[core].T
    left_t[0, :, tokens : 2 * tokens] = nleft_other[...].T
    for p in range(parts):
        left_copy(p).wait_recv()
    left_t[1, :, 0:tokens] = mleft_own[core].reshape(tokens, half_width).T
    left_t[1, :, tokens : 2 * tokens] = mleft_other[...].reshape(tokens, half_width).T
    for p in range(parts):
        right_copy(p).wait_recv()

    @pl.loop(0, tm_size)
    def _(i):
        t = turned(i + X_HI, y * X_HI, tm_size)
        yy, xh = lax.div(t, X_HI), lax.rem(t, X_HI)
        right = jnp.concatenate(
            [right_own[p, t] for p in range(parts)] + [right_other[p, t] for p in range(parts)],
            axis=0,
        )
        first = dot(left_t[0], right)
        last = (block - 1) // WIDE * WIDE
        second = dot(left_t[1], right[:, last:])
        lane = lax.broadcasted_iota(jnp.int32, second.shape, 1)
        tail = jnp.where(lane < share - last, first[:, last:], second)
        total[t, :, 0:last] = first[:, :last]
        total[t, :, last:block] = tail
        f0_send[yy, xh, :, 0:last] = first[:side_rows, :last].astype(BF16)
        f0_send[yy, xh, :, last:block] = tail[:side_rows].astype(BF16)
        f1_send[xh, yy, :, 0:last] = first[side_rows:, :last].astype(BF16)
        f1_send[xh, yy, :, last:block] = tail[side_rows:].astype(BF16)

        @pl.when(yy != y)
        def _():
            f0_copy(yy, xh).start()

        @pl.when(xh * X_LO + core != x)
        def _():
            f1_copy(yy, xh).start()

    normed_grad = dot(dqkv_ref[...], wqkv_ref[...], ((1,), (1,)))
    unit_rows = unit[...]
    gain_part = jnp.sum(normed_grad * unit_rows, axis=0, keepdims=True)
    gain_core[core] = jnp.zeros((8, WIDE), F32)
    for i in range(pairs):
        gain_core[core, i : i + 1, :] = gain_part[:, i * WIDE : (i + 1) * WIDE]

    def gain_exchange(buffer, own, count, spot, slot):
        return [
            remote(
                buffer.at[own],
                buffer.at[own],
                gain_ssem.at[slot, d],
                gain_rsem.at[slot, d],
                spot(turned(own, d, count)),
            )
            for d in range(1, count)
        ]

    def gain_sum(buffer, count):
        return functools.reduce(jnp.add, [buffer[i] for i in range(count)])

    core_gain = gain_exchange(gain_core, core, CORES, lambda cc: device(y, x, z, cc), 0)
    y_gain = gain_exchange(gain_y, y, ny, lambda yy: device(yy, x, z, core), 1)
    x_gain = gain_exchange(gain_x, x, nx, lambda xx: device(y, xx, z, core), 2)
    z_gain = gain_exchange(gain_z, z, nz, lambda zz: device(y, x, zz, core), 3)
    for move in core_gain:
        move.start()

    scaled = normed_grad * gain_ref[...]
    mean_one = jnp.mean(scaled, axis=-1, keepdims=True)
    second = jnp.mean(scaled * unit_rows, axis=-1, keepdims=True)
    back = spread[...] * (scaled - mean_one - unit_rows * second)
    fg_ref[...] = (cot_ref[...].astype(F32) + back).astype(BF16)
    mixed_out = x_ref[...].astype(F32)
    for i in range(CORES):
        mixed_half = mleft_own[i].reshape(tokens, half_width)
        mixed_out += dot(mixed_half, wout_ref[i * half_width : (i + 1) * half_width, :])
    bo_ref[...] = mixed_out.astype(BF16)

    for move in core_gain:
        move.wait_recv()
    gain_y[y] = gain_sum(gain_core, CORES)
    for move in y_gain:
        move.start()

    def n0_copy(xh):
        return remote(
            n0_send.at[xh],
            n0_recv.at[x],
            n0_ssem.at[xh],
            n0_rsem.at[x],
            device(y, xh * X_LO + core, z, core),
        )

    def n1_copy(yy):
        return remote(
            n1_send.at[yy],
            n1_recv.at[y],
            n1_ssem.at[yy],
            n1_rsem.at[y],
            device(yy, x, z, core),
        )

    def z_copy(zz):
        return remote(
            z_send.at[zz], z_recv.at[z], z_ssem.at[zz], z_rsem.at[z], device(y, x, zz, core)
        )

    def arrived(buffer, spot, sem):
        remote(buffer.at[spot], buffer.at[spot], sem.at[spot], sem.at[spot], partner).wait_recv()
        return buffer[spot].astype(F32)

    for step in range(1, X_HI + 1):
        xh = turned(x_hi, step, X_HI)
        value = total[y * X_HI + xh, 0:side_rows, :]
        for d in range(1, ny):
            value = value + arrived(f0_recv, (turned(y, d, ny), xh), f0_rsem)
        goal = xh * X_LO + core

        @pl.when(goal != x)
        def _():
            n0_send[xh] = value.astype(BF16)
            n0_copy(xh).start()

        @pl.when(goal == x)
        def _():
            n_total[0] = value

    @pl.when(active)
    def _():
        for step in range(1, ny + 1):
            yy = turned(y, step, ny)
            value = total[yy * X_HI + x_hi, side_rows : 2 * side_rows, :]
            for d in range(1, nx):
                value = value + arrived(f1_recv, (turned(x, d, nx), yy), f1_rsem)
            if step < ny:
                n1_send[yy] = value.astype(BF16)
                n1_copy(yy).start()
            else:
                n_total[1] = value

    for move in y_gain:
        move.wait_recv()
    gain_x[x] = gain_sum(gain_y, ny)
    for move in x_gain:
        move.start()

    @pl.when(active)
    def _():
        for side in range(2):
            value = n_total[side]
            for d in range(1, nx if side == 0 else ny):
                if side == 0:
                    value = value + arrived(n0_recv, turned(x, d, nx), n0_rsem)
                else:
                    value = value + arrived(n1_recv, turned(y, d, ny), n1_rsem)
            for i in range(nz // 2):
                zz = side * (nz // 2) + i
                piece = value[i * z_rows : (i + 1) * z_rows]
                z_total[zz] = piece
                z_send[zz] = piece.astype(BF16)

                @pl.when(zz != z)
                def _():
                    z_copy(zz).start()

    for move in x_gain:
        move.wait_recv()
    gain_z[z] = gain_sum(gain_x, nx)
    for move in z_gain:
        move.start()

    final = remote(final_send, final_recv, final_ssem, final_rsem, partner)

    def deliver(value):
        last = share // WIDE * WIDE
        wq_ref[:, 0:last] = value[:, :last]
        tail = value[:, last : last + WIDE]
        wq_ref[:, last:share] = tail[:, : share - last]
        if share == last:
            wo_ref[...] = tail
        else:
            count = block - share
            wo_ref[...] = pltpu.roll(tail, WIDE - (share - last), 1)[:, :count]

    @pl.when(active)
    def _():
        value = z_total[z]
        for d in range(1, nz):
            value = value + arrived(z_recv, turned(z, d, nz), z_rsem)
        value = value * inv_root
        lower = value[:final_rows]
        upper = value[final_rows:]
        final_send[...] = jnp.where(core == 0, upper, lower)
        final.start()
        deliver(jnp.where(core == 0, lower, upper))

    @pl.when(jnp.logical_not(active))
    def _():
        final.wait_recv()
        deliver(final_recv[...])

    for move in z_gain:
        move.wait_recv()
    gout_ref[...] = gain_sum(gain_z, nz) * inv_root

    normed_copy.wait_send()
    for move in core_gain + y_gain + x_gain + z_gain:
        move.wait_send()

    @pl.loop(0, parts)
    def _(p):
        for k in range(8):
            copy(p, k).wait_send()
        for j in others:
            comp_copy(p, j).wait_send()
        left_copy(p).wait_send()
        right_copy(p).wait_send()

    for xh in range(X_HI):
        for yy in range(ny):

            @pl.when(yy != y)
            def _():
                f0_copy(yy, xh).wait_send()

            @pl.when(xh * X_LO + core != x)
            def _():
                f1_copy(yy, xh).wait_send()

        @pl.when(xh * X_LO + core != x)
        def _():
            n0_copy(xh).wait_send()

    @pl.when(active)
    def _():
        for yy in range(ny):

            @pl.when(yy != y)
            def _():
                n1_copy(yy).wait_send()

        for zz in range(nz):

            @pl.when(zz != z)
            def _():
                z_copy(zz).wait_send()

        final.wait_send()


def shards(frames, norm_gain, w_qkv, w_out, cotangent):
    tm_size, inner = lax.axis_size("tm"), lax.axis_size("inner")
    width = frames.shape[-1]
    tokens = frames.shape[0] * frames.shape[1]
    frames_all = tm_size * inner
    x = frames.reshape(tokens, width)
    cot = cotangent.reshape(tokens, width)
    gain = norm_gain.reshape(1, width)
    ny, nx = tm_size // X_HI, X_HI * X_LO
    nz = inner // (X_LO * CORES)
    parts = tokens // ROWS
    half = width // CORES
    share = 3 * width // tm_size
    block = 4 * width // tm_size
    side = half // 2
    z_rows = half // nz
    final_rows = z_rows // CORES
    inv_root = 1.0 / math.sqrt(tokens * frames_all)
    sizes = (tm_size, inner, min(CLIP_MAX, frames_all), inv_root)
    vmem = pl.BlockSpec(memory_space=pltpu.VMEM)
    hbm = pl.BlockSpec(memory_space=pl.ANY)
    dma = pltpu.SemaphoreType.DMA
    block_out, frames_grad, qkv_share, out_share, gain_sum = pl.pallas_call(
        functools.partial(block_kernel, sizes),
        out_shape=(
            jax.ShapeDtypeStruct((tokens, width), BF16),
            jax.ShapeDtypeStruct((tokens, width), BF16),
            jax.ShapeDtypeStruct((final_rows, share), F32),
            jax.ShapeDtypeStruct((final_rows, block - share), F32),
            jax.ShapeDtypeStruct((8, WIDE), F32),
        ),
        in_specs=[vmem, vmem, vmem, hbm, hbm],
        out_specs=(vmem,) * 5,
        scratch_shapes=[
            pltpu.VMEM(w_qkv.shape, BF16),
            pltpu.VMEM(w_out.shape, BF16),
            pltpu.VMEM((5, parts, ROWS, 2 * width), BF16),
            pltpu.VMEM((parts, SPAN, ROWS, 4 * width), BF16),
            pltpu.VMEM((parts, SPAN, 16, WIDE), BF16),
            pltpu.VMEM((parts, SPAN, 16, WIDE), BF16),
            pltpu.VMEM((SPAN, ROWS, 2 * width), BF16),
            pltpu.VMEM((SPAN * ROWS, WIDE), BF16),
            pltpu.VMEM((tokens, 3 * width), BF16),
            pltpu.VMEM((tokens, width), F32),
            pltpu.VMEM((tokens, 1), F32),
            pltpu.VMEM((2 * WIDE, WIDE), BF16),
            pltpu.VMEM((2 * width, WIDE), BF16),
            pltpu.VMEM((WIDE, 2 * width), BF16),
            pltpu.VMEM((parts, tm_size, ROWS, block), BF16),
            pltpu.VMEM((parts, tm_size, ROWS, block), BF16),
            pltpu.VMEM((CORES, tokens, half), BF16),
            pltpu.VMEM((tokens, half), BF16),
            pltpu.VMEM((CORES, parts, ROWS, half), BF16),
            pltpu.VMEM((parts, ROWS, half), BF16),
            pltpu.VMEM((2, half, 2 * tokens), BF16),
            pltpu.VMEM((tm_size, half, block), F32),
            pltpu.VMEM((ny, X_HI, side, block), BF16),
            pltpu.VMEM((ny, X_HI, side, block), BF16),
            pltpu.VMEM((X_HI, ny, side, block), BF16),
            pltpu.VMEM((nx, ny, side, block), BF16),
            pltpu.VMEM((2, side, block), F32),
            pltpu.VMEM((X_HI, side, block), BF16),
            pltpu.VMEM((nx, side, block), BF16),
            pltpu.VMEM((ny, side, block), BF16),
            pltpu.VMEM((ny, side, block), BF16),
            pltpu.VMEM((nz, z_rows, block), F32),
            pltpu.VMEM((nz, z_rows, block), BF16),
            pltpu.VMEM((nz, z_rows, block), BF16),
            pltpu.VMEM((final_rows, block), F32),
            pltpu.VMEM((final_rows, block), F32),
            pltpu.VMEM((CORES, 8, WIDE), F32),
            pltpu.VMEM((ny, 8, WIDE), F32),
            pltpu.VMEM((nx, 8, WIDE), F32),
            pltpu.VMEM((nz, 8, WIDE), F32),
            dma((2,)),
            dma((parts, 8)),
            dma((parts, 8)),
            dma((parts, SPAN)),
            dma((parts, SPAN)),
            dma((parts, 3)),
            dma((parts, 3)),
            dma((ny, X_HI)),
            dma((ny, X_HI)),
            dma((X_HI, ny)),
            dma((nx, ny)),
            dma((X_HI,)),
            dma((nx,)),
            dma((ny,)),
            dma((ny,)),
            dma((nz,)),
            dma((nz,)),
            dma,
            dma,
            dma((4, nz)),
            dma((4, nz)),
        ],
        compiler_params=pltpu.CompilerParams(
            collective_id=0, has_side_effects=True, vmem_limit_bytes=60 * 2**20
        ),
        name="attention_block",
    )(x, gain, cot, w_qkv, w_out)
    cut = width // inner
    gain_share = lax.dynamic_slice_in_dim(
        gain_sum.reshape(-1), lax.axis_index("inner") * cut, cut
    )
    return (
        block_out.reshape(frames.shape),
        frames_grad.reshape(frames.shape),
        qkv_share,
        out_share,
        gain_share,
    )


def solution(mesh):
    in_specs = (P(("tm", "inner"), None, None), P(), P(), P(), P(("tm", "inner"), None, None))
    out_specs = (
        P(("tm", "inner"), None, None),
        P(("tm", "inner"), None, None),
        P("inner", "tm"),
        P("inner", "tm"),
        P("inner"),
    )
    return jax.shard_map(shards, mesh=mesh, in_specs=in_specs, out_specs=out_specs, check_vma=False)
```

```python
import functools
import math

import jax
import jax.numpy as jnp
from jax import lax
from jax.experimental import pallas as pl
from jax.experimental.pallas import tpu as pltpu
from jax.sharding import PartitionSpec as P

HEAD_DIM = 64
WINDOW = 4
CLIP_MAX = 256
EPSILON = 1e-06
SPAN = 2 * WINDOW + 1
WIDE = 128
ROWS = 64
CORES = 2
X_LO = 2
X_HI = 2
MESH = pl.DeviceIdType.MESH
F32 = jnp.float32
BF16 = jnp.bfloat16


def dot(a, b, dims=((1,), (0,))):
    return lax.dot_general(a, b, (dims, ((), ())), preferred_element_type=F32)


def split(wide_vals):
    high = wide_vals.astype(BF16)
    low = (wide_vals - high.astype(F32)).astype(BF16)
    return jnp.concatenate([high, low], axis=1)


def remote(source, target, ssem, rsem, where):
    return pltpu.make_async_remote_copy(
        src_ref=source,
        dst_ref=target,
        send_sem=ssem,
        recv_sem=rsem,
        device_id=where,
        device_id_type=MESH,
    )


def turned(value, step, count):
    return lax.rem(value + step, count)


def block_kernel(
    sizes,
    x_ref,
    gain_ref,
    cot_ref,
    wqkv_hbm,
    wout_hbm,
    bo_ref,
    fg_ref,
    wq_ref,
    wo_ref,
    gout_ref,
    wqkv_ref,
    wout_ref,
    xn,
    halo,
    comp,
    rcomp,
    wd,
    stack,
    dqkv_ref,
    unit,
    spread,
    ones,
    pick,
    spill,
    right_own,
    right_other,
    nleft_own,
    nleft_other,
    mleft_own,
    mleft_other,
    left_t,
    total,
    f0_send,
    f0_recv,
    f1_send,
    f1_recv,
    n_total,
    n0_send,
    n0_recv,
    n1_send,
    n1_recv,
    z_total,
    z_send,
    z_recv,
    final_send,
    final_recv,
    gain_core,
    gain_y,
    gain_x,
    gain_z,
    gain_last,
    load_sem,
    send_sem,
    recv_sem,
    csend_sem,
    crecv_sem,
    gsend_sem,
    grecv_sem,
    f0_ssem,
    f0_rsem,
    f1_ssem,
    f1_rsem,
    n0_ssem,
    n0_rsem,
    n1_ssem,
    n1_rsem,
    z_ssem,
    z_rsem,
    final_ssem,
    final_rsem,
    gain_ssem,
    gain_rsem,
):
    tm_size, inner, clip, inv_root = sizes
    frames_all = tm_size * inner
    tokens, width = x_ref.shape
    pairs = width // WIDE
    parts = tokens // ROWS
    ny, nx = tm_size // X_HI, X_HI * X_LO
    nz = inner // (X_LO * CORES)
    half_width = width // CORES
    share = 3 * width // tm_size
    block = 4 * width // tm_size
    side_rows = half_width // 2
    z_rows = half_width // nz
    final_rows = z_rows // CORES

    tm_at = lax.axis_index("tm")
    inner_at = lax.axis_index("inner")
    f = tm_at * inner + inner_at
    odd = lax.rem(f, 2)
    core = lax.rem(inner_at, CORES)
    z = lax.rem(lax.div(inner_at, CORES), nz)
    x_lo = lax.div(inner_at, CORES * nz)
    x_hi = lax.rem(tm_at, X_HI)
    x = x_hi * X_LO + x_lo
    y = lax.div(tm_at, X_HI)
    active = x_lo == core

    def at(offset):
        g = lax.rem(f + offset + frames_all, frames_all)
        return (lax.div(g, inner), lax.rem(g, inner))

    def device(yy, xx, zz, cc):
        return (
            yy * X_HI + lax.div(xx, X_LO),
            (lax.rem(xx, X_LO) * nz + zz) * CORES + cc,
        )

    partner = device(y, x, z, 1 - core)
    others = [j for j in range(-WINDOW, WINDOW + 1) if j != 0]
    peers = [at(j) for j in others]
    peers += [device(turned(y, d, ny), x, z, core) for d in range(1, ny)]
    peers += [device(y, turned(x, d, nx), z, core) for d in range(1, nx)]
    peers += [device(y, x, turned(z, d, nz), core) for d in range(1, nz)]
    barrier = pltpu.get_barrier_semaphore()
    for peer in peers:
        pl.semaphore_signal(barrier, inc=1, device_id=peer, device_id_type=MESH)

    load_qkv = pltpu.make_async_copy(wqkv_hbm, wqkv_ref, load_sem.at[0])
    load_out = pltpu.make_async_copy(wout_hbm, wout_ref, load_sem.at[1])
    load_qkv.start()
    load_out.start()

    wide_vals = x_ref[...].astype(F32)
    center = wide_vals - jnp.mean(wide_vals, axis=-1, keepdims=True)
    spread_one = lax.rsqrt(jnp.mean(center * center, axis=-1, keepdims=True) + EPSILON)
    unit_rows = center * spread_one
    unit[...] = unit_rows
    spread[...] = spread_one
    gain_row = gain_ref[...].reshape(1, width)
    normed = (unit_rows * gain_row).astype(BF16)
    for p in range(parts):
        rows = slice(p * ROWS, (p + 1) * ROWS)
        xn[2, p, :, 0:width] = normed[rows]
        xn[2, p, :, width : 2 * width] = cot_ref[rows, :]
    for i in range(CORES):
        nleft_own[i] = normed[:, i * half_width : (i + 1) * half_width]

    def columns(c, part, size=WIDE):
        return pl.ds(pl.multiple_of(part * width + c * size, size), size)

    def copy(p, k):
        if k < 4:
            source = xn.at[(2, 2, 1, 3)[k], p]
            target = xn.at[(1, 3, 0, 4)[k], p]
            where = at((2, -2, 2, -2)[k])
        else:
            slot = (4, 2, 6, 8 - 8 * odd)[k - 4]
            source = halo.at[p, slot]
            target = halo.at[p, slot - 1 + 2 * odd]
            where = partner
        return remote(source, target, send_sem.at[p, k], recv_sem.at[p, k], where)

    def comp_copy(p, j):
        k = j + WINDOW
        return remote(
            comp.at[p, k],
            rcomp.at[p, SPAN - 1 - k],
            csend_sem.at[p, k],
            crecv_sem.at[p, k],
            at(j),
        )

    normed_copy = remote(
        nleft_own.at[1 - core], nleft_other, gsend_sem.at[0, 2], grecv_sem.at[0, 2], partner
    )

    def left_copy(p):
        return remote(
            mleft_own.at[1 - core, p],
            mleft_other.at[p],
            gsend_sem.at[p, 0],
            grecv_sem.at[p, 0],
            partner,
        )

    def right_copy(p):
        return remote(
            right_own.at[p], right_other.at[p], gsend_sem.at[p, 1], grecv_sem.at[p, 1], partner
        )

    pl.semaphore_wait(barrier, len(peers))

    @pl.loop(0, min(2, parts))
    def _(p):
        copy(p, 0).start()
        copy(p, 1).start()

    normed_copy.start()

    row_at = lax.broadcasted_iota(jnp.int32, (2 * WIDE, WIDE), 0)
    lane_at = lax.broadcasted_iota(jnp.int32, (2 * WIDE, WIDE), 1)
    same = (lax.rem(row_at, WIDE) // HEAD_DIM) == (lane_at // HEAD_DIM)
    ones[...] = jnp.where(same, 1.0, 0.0).astype(BF16)
    row_at = lax.broadcasted_iota(jnp.int32, pick.shape, 0)
    lane_at = lax.broadcasted_iota(jnp.int32, pick.shape, 1)
    pick[...] = jnp.where(row_at == lane_at * HEAD_DIM, 1.0, 0.0).astype(BF16)
    row_at = lax.broadcasted_iota(jnp.int32, spill.shape, 0)
    lane_at = lax.broadcasted_iota(jnp.int32, spill.shape, 1)
    spill[...] = jnp.where(lane_at // HEAD_DIM == row_at, 1.0, 0.0).astype(BF16)

    def place(p, value, start, stride, lead):
        left = value.shape[1]
        taken = 0
        while taken < left:
            t = (start + taken) // stride
            into = start + taken - t * stride
            count = min(left - taken, stride - into)
            right_own[p, t, :, lead + into : lead + into + count] = value[:, taken : taken + count]
            taken += count

    for p in range(parts):
        for m in range(pairs):
            value = cot_ref[p * ROWS : (p + 1) * ROWS, m * WIDE : (m + 1) * WIDE]
            place(p, value, m * WIDE, width // tm_size, share)

    load_qkv.wait()
    load_out.wait()

    def project(rows_in, put):
        for part in range(3):
            weight = wqkv_ref[:, part * width : (part + 1) * width]
            put(part, dot(rows_in[:, 0:width], weight).astype(BF16))
        put(3, dot(rows_in[:, width : 2 * width], wout_ref[...], ((1,), (1,))).astype(BF16))

    def put_own(part, value):
        for p in range(parts):
            halo[p, 4, :, part * width : (part + 1) * width] = value[p * ROWS : (p + 1) * ROWS]

    project(xn[2].reshape(tokens, 2 * width), put_own)

    @pl.loop(0, parts)
    def _(p):
        copy(p, 4).start()

    def relay(p):
        copy(p, 0).wait_recv()
        copy(p, 2).start()
        copy(p, 1).wait_recv()
        copy(p, 3).start()

    def project_others(p):
        copy(p, 2).wait_recv()
        copy(p, 3).wait_recv()
        rows_in = jnp.concatenate([xn[1, p], xn[3, p], xn[0, p], xn[4, p]], axis=0)

        def put(part, value):
            for i, k in enumerate((2, 6, 0, 8)):
                halo[p, k, :, part * width : (part + 1) * width] = value[
                    i * ROWS : (i + 1) * ROWS
                ]

        project(rows_in, put)
        for k in (5, 6, 7):
            copy(p, k).start()

    def attend(p):
        for k in (4, 5, 6, 7):
            copy(p, k).wait_recv()
        rows = pl.ds(pl.multiple_of(p * ROWS, ROWS), ROWS)

        @pl.loop(0, pairs)
        def _(c):
            def load(k, part):
                return halo[p, k, :, columns(c, part)].astype(F32)

            query = load(4, 0)
            grad = halo[p, 4, :, columns(c, 3)]
            products = [split(query * load(k, 1)) for k in range(SPAN)]
            scores = dot(jnp.concatenate(products, axis=0), ones[...]) * (HEAD_DIM**-0.5)
            products = [grad * halo[p, k, :, columns(c, 2)] for k in range(SPAN)]
            dots = dot(jnp.concatenate(products, axis=0), ones[0:WIDE])
            score = []
            for k in range(SPAN):
                g = f + (k - WINDOW)
                inside = (g >= 0) & (g < frames_all)
                inside = inside & (lax.div(g + clip, clip) == lax.div(f + clip, clip))
                cap = jnp.where(inside, 3e38, -1e30).astype(F32)
                score.append(jnp.minimum(scores[k * ROWS : (k + 1) * ROWS], cap))
            top = functools.reduce(jnp.maximum, score)
            raised = [jnp.exp(s - top) for s in score]
            scale = 1.0 / functools.reduce(jnp.add, raised)
            soft = [e * scale for e in raised]
            mixed = jnp.zeros((ROWS, WIDE), F32)
            centre = jnp.zeros((ROWS, WIDE), F32)
            weight_at = pl.ds(pl.multiple_of(c * 2 * WIDE, WIDE), WIDE)
            slope_at = pl.ds(pl.multiple_of(c * 2 * WIDE + WIDE, WIDE), WIDE)
            for k in range(SPAN):
                weight = soft[k].astype(BF16)
                wd[k, :, weight_at] = weight
                mixed += weight.astype(F32) * load(k, 2)
                centre += soft[k] * dots[k * ROWS : (k + 1) * ROWS]
            side = lax.div(c, pairs // CORES)
            mleft_own[side, p, :, columns(lax.rem(c, pairs // CORES), 0)] = mixed.astype(BF16)
            query_grad = jnp.zeros((ROWS, WIDE), F32)
            for k in range(SPAN):
                gap = dots[k * ROWS : (k + 1) * ROWS] - centre
                slope = (soft[k] * gap * (HEAD_DIM**-0.5)).astype(BF16)
                wd[k, :, slope_at] = slope
                query_grad += slope.astype(F32) * load(k, 1)
            dqkv_ref[rows, columns(c, 0)] = query_grad.astype(BF16)

        small = dot(wd[...].reshape(SPAN * ROWS, 2 * width), pick[...])
        for k in range(SPAN):
            packed = small[k * ROWS : k * ROWS + 16]
            for r in range(1, ROWS // 16):
                at_row = k * ROWS + r * 16
                packed += pltpu.roll(small[at_row : at_row + 16], 32 * r, 1)
            if k == WINDOW:
                rcomp[p, k] = packed.astype(BF16)
            else:
                comp[p, k] = packed.astype(BF16)
                comp_copy(p, k - WINDOW).start()

    def collect(p):
        for j in others:
            comp_copy(p, j).wait_recv()
        rows = pl.ds(pl.multiple_of(p * ROWS, ROWS), ROWS)
        for k in range(SPAN):
            packed = rcomp[p, k].astype(F32)
            for r in range(ROWS // 16):
                value = packed if r == 0 else pltpu.roll(packed, WIDE - 32 * r, 1)
                stack[k * ROWS + r * 16 : k * ROWS + (r + 1) * 16, :] = value.astype(BF16)

        @pl.loop(0, pairs)
        def _(c):
            wide = dot(stack[...], spill[:, columns(c, 0, 2 * WIDE)])
            key_grad = jnp.zeros((ROWS, WIDE), F32)
            value_grad = jnp.zeros((ROWS, WIDE), F32)
            for k in range(SPAN):
                piece = wide[k * ROWS : (k + 1) * ROWS]
                value_grad += piece[:, :WIDE] * halo[p, k, :, columns(c, 3)].astype(F32)
                key_grad += piece[:, WIDE:] * halo[p, k, :, columns(c, 0)].astype(F32)
            dqkv_ref[rows, columns(c, 1)] = key_grad.astype(BF16)
            dqkv_ref[rows, columns(c, 2)] = value_grad.astype(BF16)

        for m in range(3 * pairs):
            value = dqkv_ref[rows, m * WIDE : (m + 1) * WIDE]
            place(p, value, m * WIDE, share, 0)
        left_copy(p).start()
        right_copy(p).start()

    def start_own(p):
        copy(p, 0).start()
        copy(p, 1).start()

    relay(0)
    start_own(2)
    relay(1)
    start_own(3)
    project_others(0)

    @pl.loop(0, parts)
    def _(p):
        @pl.when(p == 0)
        def _():
            relay(2)

        attend(p)

        @pl.when(p == 0)
        def _():
            relay(3)

        @pl.when(p + 1 < parts)
        def _():
            project_others(p + 1)

        @pl.when(p > 0)
        def _():
            collect(p - 1)

    collect(parts - 1)

    def f0_copy(yy, xh):
        return remote(
            f0_send.at[yy, xh],
            f0_recv.at[y, xh],
            f0_ssem.at[yy, xh],
            f0_rsem.at[y, xh],
            device(yy, x, z, core),
        )

    def f1_copy(yy, xh):
        return remote(
            f1_send.at[xh, yy],
            f1_recv.at[x, yy],
            f1_ssem.at[xh, yy],
            f1_rsem.at[x, yy],
            device(y, xh * X_LO + core, z, core),
        )

    normed_copy.wait_recv()
    left_t[0, :, 0:tokens] = nleft_own[core].T
    left_t[0, :, tokens : 2 * tokens] = nleft_other[...].T
    for p in range(parts):
        left_copy(p).wait_recv()
    left_t[1, :, 0:tokens] = mleft_own[core].reshape(tokens, half_width).T
    left_t[1, :, tokens : 2 * tokens] = mleft_other[...].reshape(tokens, half_width).T
    for p in range(parts):
        right_copy(p).wait_recv()

    @pl.loop(0, tm_size)
    def _(i):
        t = turned(i + X_HI, y * X_HI, tm_size)
        yy, xh = lax.div(t, X_HI), lax.rem(t, X_HI)
        right = jnp.concatenate(
            [right_own[p, t] for p in range(parts)] + [right_other[p, t] for p in range(parts)],
            axis=0,
        )
        first = dot(left_t[0], right)
        last = (block - 1) // WIDE * WIDE
        second = dot(left_t[1], right[:, last:])
        lane = lax.broadcasted_iota(jnp.int32, second.shape, 1)
        tail = jnp.where(lane < share - last, first[:, last:], second)
        total[t, :, 0:last] = first[:, :last]
        total[t, :, last:block] = tail
        f0_send[yy, xh, :, 0:last] = first[:side_rows, :last].astype(BF16)
        f0_send[yy, xh, :, last:block] = tail[:side_rows].astype(BF16)
        f1_send[xh, yy, :, 0:last] = first[side_rows:, :last].astype(BF16)
        f1_send[xh, yy, :, last:block] = tail[side_rows:].astype(BF16)

        @pl.when(yy != y)
        def _():
            f0_copy(yy, xh).start()

        @pl.when(xh * X_LO + core != x)
        def _():
            f1_copy(yy, xh).start()

    normed_grad = dot(dqkv_ref[...], wqkv_ref[...], ((1,), (1,)))
    unit_rows = unit[...]
    gain_part = jnp.sum(normed_grad * unit_rows, axis=0, keepdims=True)
    gain_core[core] = jnp.zeros((8, WIDE), F32)
    for i in range(pairs):
        gain_core[core, i : i + 1, :] = gain_part[:, i * WIDE : (i + 1) * WIDE]

    def gain_exchange(buffer, own, count, spot, slot):
        return [
            remote(
                buffer.at[own],
                buffer.at[own],
                gain_ssem.at[slot, d],
                gain_rsem.at[slot, d],
                spot(turned(own, d, count)),
            )
            for d in range(1, count)
        ]

    def gain_sum(buffer, count):
        return functools.reduce(jnp.add, [buffer[i] for i in range(count)])

    core_gain = gain_exchange(gain_core, core, CORES, lambda cc: device(y, x, z, cc), 0)
    y_gain = gain_exchange(gain_y, y, ny, lambda yy: device(yy, x, z, core), 1)
    x_gain = gain_exchange(gain_x, x, nx, lambda xx: device(y, xx, z, core), 2)
    z_gain = gain_exchange(gain_z, z, nz, lambda zz: device(y, x, zz, core), 3)
    for move in core_gain:
        move.start()

    scaled = normed_grad * gain_ref[...].reshape(1, width)
    mean_one = jnp.mean(scaled, axis=-1, keepdims=True)
    second = jnp.mean(scaled * unit_rows, axis=-1, keepdims=True)
    back = spread[...] * (scaled - mean_one - unit_rows * second)
    fg_ref[...] = (cot_ref[...].astype(F32) + back).astype(BF16)
    mixed_out = x_ref[...].astype(F32)
    for i in range(CORES):
        mixed_half = mleft_own[i].reshape(tokens, half_width)
        mixed_out += dot(mixed_half, wout_ref[i * half_width : (i + 1) * half_width, :])
    bo_ref[...] = mixed_out.astype(BF16)

    for move in core_gain:
        move.wait_recv()
    gain_y[y] = gain_sum(gain_core, CORES)
    for move in y_gain:
        move.start()

    def n0_copy(xh):
        return remote(
            n0_send.at[xh],
            n0_recv.at[x],
            n0_ssem.at[xh],
            n0_rsem.at[x],
            device(y, xh * X_LO + core, z, core),
        )

    def n1_copy(yy):
        return remote(
            n1_send.at[yy],
            n1_recv.at[y],
            n1_ssem.at[yy],
            n1_rsem.at[y],
            device(yy, x, z, core),
        )

    def z_copy(zz):
        return remote(
            z_send.at[zz], z_recv.at[z], z_ssem.at[zz], z_rsem.at[z], device(y, x, zz, core)
        )

    def arrived(buffer, spot, sem):
        remote(buffer.at[spot], buffer.at[spot], sem.at[spot], sem.at[spot], partner).wait_recv()
        return buffer[spot].astype(F32)

    for step in range(1, X_HI + 1):
        xh = turned(x_hi, step, X_HI)
        value = total[y * X_HI + xh, 0:side_rows, :]
        for d in range(1, ny):
            value = value + arrived(f0_recv, (turned(y, d, ny), xh), f0_rsem)
        goal = xh * X_LO + core

        @pl.when(goal != x)
        def _():
            n0_send[xh] = value.astype(BF16)
            n0_copy(xh).start()

        @pl.when(goal == x)
        def _():
            n_total[0] = value

    @pl.when(active)
    def _():
        for step in range(1, ny + 1):
            yy = turned(y, step, ny)
            value = total[yy * X_HI + x_hi, side_rows : 2 * side_rows, :]
            for d in range(1, nx):
                value = value + arrived(f1_recv, (turned(x, d, nx), yy), f1_rsem)
            if step < ny:
                n1_send[yy] = value.astype(BF16)
                n1_copy(yy).start()
            else:
                n_total[1] = value

    for move in y_gain:
        move.wait_recv()
    gain_x[x] = gain_sum(gain_y, ny)
    for move in x_gain:
        move.start()

    @pl.when(active)
    def _():
        for side in range(2):
            value = n_total[side]
            for d in range(1, nx if side == 0 else ny):
                if side == 0:
                    value = value + arrived(n0_recv, turned(x, d, nx), n0_rsem)
                else:
                    value = value + arrived(n1_recv, turned(y, d, ny), n1_rsem)
            for i in range(nz // 2):
                zz = side * (nz // 2) + i
                piece = value[i * z_rows : (i + 1) * z_rows]
                z_total[zz] = piece
                z_send[zz] = piece.astype(BF16)

                @pl.when(zz != z)
                def _():
                    z_copy(zz).start()

    for move in x_gain:
        move.wait_recv()
    gain_z[z] = gain_sum(gain_x, nx)
    for move in z_gain:
        move.start()

    final = remote(final_send, final_recv, final_ssem, final_rsem, partner)

    def deliver(value):
        last = share // WIDE * WIDE
        wq_ref[:, 0:last] = value[:, :last]
        tail = value[:, last : last + WIDE]
        wq_ref[:, last:share] = tail[:, : share - last]
        if share == last:
            wo_ref[...] = tail
        else:
            count = block - share
            wo_ref[...] = pltpu.roll(tail, WIDE - (share - last), 1)[:, :count]

    @pl.when(active)
    def _():
        value = z_total[z]
        for d in range(1, nz):
            value = value + arrived(z_recv, turned(z, d, nz), z_rsem)
        value = value * inv_root
        lower = value[:final_rows]
        upper = value[final_rows:]
        final_send[...] = jnp.where(core == 0, upper, lower)
        final.start()
        deliver(jnp.where(core == 0, lower, upper))

    @pl.when(jnp.logical_not(active))
    def _():
        final.wait_recv()
        deliver(final_recv[...])

    for move in z_gain:
        move.wait_recv()
    gain_last[...] = gain_sum(gain_z, nz) * inv_root
    cut = width // inner
    row_one = lax.div(inner_at * cut, WIDE)
    lead = lax.rem(inner_at * cut, WIDE)
    low = jnp.broadcast_to(gain_last[pl.ds(row_one, 1), :], (8, WIDE))
    high = jnp.broadcast_to(gain_last[pl.ds(row_one + 1, 1), :], (8, WIDE))
    lane = lax.broadcasted_iota(jnp.int32, (8, WIDE), 1)
    shift = lax.rem(WIDE - lead, WIDE)
    merged = jnp.where(
        lane < WIDE - lead, pltpu.roll(low, shift, 1), pltpu.roll(high, shift, 1)
    )
    gout_ref[...] = merged[0:1, :cut]

    normed_copy.wait_send()
    for move in core_gain + y_gain + x_gain + z_gain:
        move.wait_send()

    @pl.loop(0, parts)
    def _(p):
        for k in range(8):
            copy(p, k).wait_send()
        for j in others:
            comp_copy(p, j).wait_send()
        left_copy(p).wait_send()
        right_copy(p).wait_send()

    for xh in range(X_HI):
        for yy in range(ny):

            @pl.when(yy != y)
            def _():
                f0_copy(yy, xh).wait_send()

            @pl.when(xh * X_LO + core != x)
            def _():
                f1_copy(yy, xh).wait_send()

        @pl.when(xh * X_LO + core != x)
        def _():
            n0_copy(xh).wait_send()

    @pl.when(active)
    def _():
        for yy in range(ny):

            @pl.when(yy != y)
            def _():
                n1_copy(yy).wait_send()

        for zz in range(nz):

            @pl.when(zz != z)
            def _():
                z_copy(zz).wait_send()

        final.wait_send()


def copy_kernel(*refs):
    count = len(refs) // 2
    for source, target in zip(refs[:count], refs[count:], strict=True):
        target[...] = source[...].reshape(target.shape)


def hand_over(*arrays):
    vmem = pl.BlockSpec(memory_space=pltpu.VMEM)
    shapes = [a.shape for a in arrays[:-1]] + [(arrays[-1].size,)]
    return pl.pallas_call(
        copy_kernel,
        out_shape=tuple(
            jax.ShapeDtypeStruct(shape, a.dtype) for shape, a in zip(shapes, arrays, strict=True)
        ),
        in_specs=[vmem] * len(arrays),
        out_specs=(vmem,) * len(arrays),
        name="hand_over",
    )(*arrays)


def shards(frames, norm_gain, w_qkv, w_out, cotangent):
    tm_size, inner = lax.axis_size("tm"), lax.axis_size("inner")
    width = frames.shape[-1]
    tokens = frames.shape[0] * frames.shape[1]
    frames_all = tm_size * inner
    x = frames.reshape(tokens, width)
    cot = cotangent.reshape(tokens, width)
    ny, nx = tm_size // X_HI, X_HI * X_LO
    nz = inner // (X_LO * CORES)
    parts = tokens // ROWS
    half = width // CORES
    share = 3 * width // tm_size
    block = 4 * width // tm_size
    side = half // 2
    z_rows = half // nz
    final_rows = z_rows // CORES
    inv_root = 1.0 / math.sqrt(tokens * frames_all)
    sizes = (tm_size, inner, min(CLIP_MAX, frames_all), inv_root)
    vmem = pl.BlockSpec(memory_space=pltpu.VMEM)
    hbm = pl.BlockSpec(memory_space=pl.ANY)
    dma = pltpu.SemaphoreType.DMA
    block_out, frames_grad, qkv_share, out_share, gain_sum = pl.pallas_call(
        functools.partial(block_kernel, sizes),
        out_shape=(
            jax.ShapeDtypeStruct((tokens, width), BF16),
            jax.ShapeDtypeStruct((tokens, width), BF16),
            jax.ShapeDtypeStruct((final_rows, share), F32),
            jax.ShapeDtypeStruct((final_rows, block - share), F32),
            jax.ShapeDtypeStruct((1, width // inner), F32),
        ),
        in_specs=[vmem, vmem, vmem, hbm, hbm],
        out_specs=(vmem,) * 5,
        scratch_shapes=[
            pltpu.VMEM(w_qkv.shape, BF16),
            pltpu.VMEM(w_out.shape, BF16),
            pltpu.VMEM((5, parts, ROWS, 2 * width), BF16),
            pltpu.VMEM((parts, SPAN, ROWS, 4 * width), BF16),
            pltpu.VMEM((parts, SPAN, 16, WIDE), BF16),
            pltpu.VMEM((parts, SPAN, 16, WIDE), BF16),
            pltpu.VMEM((SPAN, ROWS, 2 * width), BF16),
            pltpu.VMEM((SPAN * ROWS, WIDE), BF16),
            pltpu.VMEM((tokens, 3 * width), BF16),
            pltpu.VMEM((tokens, width), F32),
            pltpu.VMEM((tokens, 1), F32),
            pltpu.VMEM((2 * WIDE, WIDE), BF16),
            pltpu.VMEM((2 * width, WIDE), BF16),
            pltpu.VMEM((WIDE, 2 * width), BF16),
            pltpu.VMEM((parts, tm_size, ROWS, block), BF16),
            pltpu.VMEM((parts, tm_size, ROWS, block), BF16),
            pltpu.VMEM((CORES, tokens, half), BF16),
            pltpu.VMEM((tokens, half), BF16),
            pltpu.VMEM((CORES, parts, ROWS, half), BF16),
            pltpu.VMEM((parts, ROWS, half), BF16),
            pltpu.VMEM((2, half, 2 * tokens), BF16),
            pltpu.VMEM((tm_size, half, block), F32),
            pltpu.VMEM((ny, X_HI, side, block), BF16),
            pltpu.VMEM((ny, X_HI, side, block), BF16),
            pltpu.VMEM((X_HI, ny, side, block), BF16),
            pltpu.VMEM((nx, ny, side, block), BF16),
            pltpu.VMEM((2, side, block), F32),
            pltpu.VMEM((X_HI, side, block), BF16),
            pltpu.VMEM((nx, side, block), BF16),
            pltpu.VMEM((ny, side, block), BF16),
            pltpu.VMEM((ny, side, block), BF16),
            pltpu.VMEM((nz, z_rows, block), F32),
            pltpu.VMEM((nz, z_rows, block), BF16),
            pltpu.VMEM((nz, z_rows, block), BF16),
            pltpu.VMEM((final_rows, block), F32),
            pltpu.VMEM((final_rows, block), F32),
            pltpu.VMEM((CORES, 8, WIDE), F32),
            pltpu.VMEM((ny, 8, WIDE), F32),
            pltpu.VMEM((nx, 8, WIDE), F32),
            pltpu.VMEM((nz, 8, WIDE), F32),
            pltpu.VMEM((8, WIDE), F32),
            dma((2,)),
            dma((parts, 8)),
            dma((parts, 8)),
            dma((parts, SPAN)),
            dma((parts, SPAN)),
            dma((parts, 3)),
            dma((parts, 3)),
            dma((ny, X_HI)),
            dma((ny, X_HI)),
            dma((X_HI, ny)),
            dma((nx, ny)),
            dma((X_HI,)),
            dma((nx,)),
            dma((ny,)),
            dma((ny,)),
            dma((nz,)),
            dma((nz,)),
            dma,
            dma,
            dma((4, nz)),
            dma((4, nz)),
        ],
        compiler_params=pltpu.CompilerParams(
            collective_id=0, has_side_effects=True, vmem_limit_bytes=60 * 2**20
        ),
        name="attention_block",
    )(x, norm_gain, cot, w_qkv, w_out)
    outs = hand_over(block_out, frames_grad, qkv_share, out_share, gain_sum)
    return (
        outs[0].reshape(frames.shape),
        outs[1].reshape(frames.shape),
        outs[2],
        outs[3],
        outs[4],
    )


def solution(mesh):
    in_specs = (P(("tm", "inner"), None, None), P(), P(), P(), P(("tm", "inner"), None, None))
    out_specs = (
        P(("tm", "inner"), None, None),
        P(("tm", "inner"), None, None),
        P("inner", "tm"),
        P("inner", "tm"),
        P("inner"),
    )
    return jax.shard_map(shards, mesh=mesh, in_specs=in_specs, out_specs=out_specs, check_vma=False)
```

```python
import functools
import math

import jax
import jax.numpy as jnp
from jax import lax
from jax.experimental import pallas as pl
from jax.experimental.pallas import tpu as pltpu
from jax.sharding import PartitionSpec as P

HEAD_DIM = 64
WINDOW = 4
CLIP_MAX = 256
EPSILON = 1e-06
SPAN = 2 * WINDOW + 1
WIDE = 128
ROWS = 64
COPIES = 17
CORES = 2
X_LO = 2
X_HI = 2
MESH = pl.DeviceIdType.MESH
F32 = jnp.float32
BF16 = jnp.bfloat16


def dot(a, b, dims=((1,), (0,))):
    return lax.dot_general(a, b, (dims, ((), ())), preferred_element_type=F32)


def split(wide_vals):
    high = wide_vals.astype(BF16)
    low = (wide_vals - high.astype(F32)).astype(BF16)
    return jnp.concatenate([high, low], axis=1)


def remote(source, target, ssem, rsem, where):
    return pltpu.make_async_remote_copy(
        src_ref=source,
        dst_ref=target,
        send_sem=ssem,
        recv_sem=rsem,
        device_id=where,
        device_id_type=MESH,
    )


def turned(value, step, count):
    return lax.rem(value + step, count)


def block_kernel(
    sizes,
    x_ref,
    gain_ref,
    cot_ref,
    wqkv_hbm,
    wout_hbm,
    bo_ref,
    fg_ref,
    wq_ref,
    wo_ref,
    gout_ref,
    wqkv_ref,
    wout_ref,
    xn,
    halo,
    comp,
    rcomp,
    wd,
    stack,
    dqkv_ref,
    unit,
    spread,
    ones,
    pick,
    spill,
    right_own,
    right_other,
    nleft_own,
    nleft_other,
    mleft_own,
    mleft_other,
    left_t,
    total,
    f0_send,
    f0_recv,
    f1_send,
    f1_recv,
    n_total,
    n0_send,
    n0_recv,
    n1_send,
    n1_recv,
    z_total,
    z_send,
    z_recv,
    final_send,
    final_recv,
    gain_core,
    gain_y,
    gain_x,
    gain_z,
    gain_last,
    load_sem,
    send_sem,
    recv_sem,
    csend_sem,
    crecv_sem,
    gsend_sem,
    grecv_sem,
    f0_ssem,
    f0_rsem,
    f1_ssem,
    f1_rsem,
    n0_ssem,
    n0_rsem,
    n1_ssem,
    n1_rsem,
    z_ssem,
    z_rsem,
    final_ssem,
    final_rsem,
    gain_ssem,
    gain_rsem,
):
    tm_size, inner, clip, inv_root = sizes
    frames_all = tm_size * inner
    tokens, width = x_ref.shape
    pairs = width // WIDE
    parts = tokens // ROWS
    ny, nx = tm_size // X_HI, X_HI * X_LO
    nz = inner // (X_LO * CORES)
    half_width = width // CORES
    share = 3 * width // tm_size
    block = 4 * width // tm_size
    side_rows = half_width // 2
    z_rows = half_width // nz
    final_rows = z_rows // CORES

    tm_at = lax.axis_index("tm")
    inner_at = lax.axis_index("inner")
    f = tm_at * inner + inner_at
    odd = lax.rem(f, 2)
    core = lax.rem(inner_at, CORES)
    z = lax.rem(lax.div(inner_at, CORES), nz)
    x_lo = lax.div(inner_at, CORES * nz)
    x_hi = lax.rem(tm_at, X_HI)
    x = x_hi * X_LO + x_lo
    y = lax.div(tm_at, X_HI)
    active = x_lo == core

    def at(offset):
        g = lax.rem(f + offset + frames_all, frames_all)
        return (lax.div(g, inner), lax.rem(g, inner))

    def device(yy, xx, zz, cc):
        return (
            yy * X_HI + lax.div(xx, X_LO),
            (lax.rem(xx, X_LO) * nz + zz) * CORES + cc,
        )

    partner = device(y, x, z, 1 - core)
    others = [j for j in range(-WINDOW, WINDOW + 1) if j != 0]
    peers = [at(j) for j in others]
    peers += [device(turned(y, d, ny), x, z, core) for d in range(1, ny)]
    peers += [device(y, turned(x, d, nx), z, core) for d in range(1, nx)]
    peers += [device(y, x, turned(z, d, nz), core) for d in range(1, nz)]
    barrier = pltpu.get_barrier_semaphore()
    for peer in peers:
        pl.semaphore_signal(barrier, inc=1, device_id=peer, device_id_type=MESH)

    load_qkv = pltpu.make_async_copy(wqkv_hbm, wqkv_ref, load_sem.at[0])
    load_out = pltpu.make_async_copy(wout_hbm, wout_ref, load_sem.at[1])
    load_qkv.start()
    load_out.start()

    def normalize(p):
        rows = slice(p * ROWS, (p + 1) * ROWS)
        wide_vals = x_ref[rows, :].astype(F32)
        center = wide_vals - jnp.mean(wide_vals, axis=-1, keepdims=True)
        variance = jnp.mean(center * center, axis=-1, keepdims=True)
        spread_one = lax.rsqrt(variance + EPSILON)
        unit_rows = center * spread_one
        unit[rows, :] = unit_rows
        spread[rows, :] = spread_one
        normed = (unit_rows * gain_ref[...].reshape(1, width)).astype(BF16)
        xn[2, p, :, 0:width] = normed
        xn[2, p, :, width : 2 * width] = cot_ref[rows, :]
        for i in range(CORES):
            nleft_own[i, rows, :] = normed[:, i * half_width : (i + 1) * half_width]

    normalize(0)

    def columns(c, part, size=WIDE):
        return pl.ds(pl.multiple_of(part * width + c * size, size), size)

    def copy(p, k):
        if k < 4:
            source = xn.at[(2, 2, 1, 3)[k], p]
            target = xn.at[(1, 3, 0, 4)[k], p]
            where = at((2, -2, 2, -2)[k])
        elif k == 4:
            source = halo.at[p, 4]
            target = halo.at[p, 3 + 2 * odd]
            where = partner
        else:
            slot = (2, 6, 8 - 8 * odd)[(k - 5) % 3]
            part = (k - 5) // 3
            lanes = pl.ds(part * width, width)
            source = halo.at[p, slot, :, lanes]
            target = halo.at[p, slot - 1 + 2 * odd, :, lanes]
            where = partner
        return remote(source, target, send_sem.at[p, k], recv_sem.at[p, k], where)

    def comp_copy(p, j):
        k = j + WINDOW
        return remote(
            comp.at[p, k],
            rcomp.at[p, SPAN - 1 - k],
            csend_sem.at[p, k],
            crecv_sem.at[p, k],
            at(j),
        )

    normed_copy = remote(
        nleft_own.at[1 - core], nleft_other, gsend_sem.at[0, 2], grecv_sem.at[0, 2], partner
    )

    def left_copy(p):
        return remote(
            mleft_own.at[1 - core, p],
            mleft_other.at[p],
            gsend_sem.at[p, 0],
            grecv_sem.at[p, 0],
            partner,
        )

    def right_copy(p):
        return remote(
            right_own.at[p], right_other.at[p], gsend_sem.at[p, 1], grecv_sem.at[p, 1], partner
        )

    pl.semaphore_wait(barrier, len(peers))

    def start_own(p):
        copy(p, 0).start()
        copy(p, 1).start()

    start_own(0)
    normalize(1)
    start_own(1)
    for p in range(2, parts):
        normalize(p)
    normed_copy.start()

    row_at = lax.broadcasted_iota(jnp.int32, (2 * WIDE, WIDE), 0)
    lane_at = lax.broadcasted_iota(jnp.int32, (2 * WIDE, WIDE), 1)
    same = (lax.rem(row_at, WIDE) // HEAD_DIM) == (lane_at // HEAD_DIM)
    ones[...] = jnp.where(same, HEAD_DIM**-0.5, 0.0).astype(BF16)
    row_at = lax.broadcasted_iota(jnp.int32, pick.shape, 0)
    lane_at = lax.broadcasted_iota(jnp.int32, pick.shape, 1)
    pick[...] = jnp.where(row_at == lane_at * HEAD_DIM, 1.0, 0.0).astype(BF16)
    row_at = lax.broadcasted_iota(jnp.int32, spill.shape, 0)
    lane_at = lax.broadcasted_iota(jnp.int32, spill.shape, 1)
    spill[...] = jnp.where(lane_at // HEAD_DIM == row_at, 1.0, 0.0).astype(BF16)

    def place(p, value, start, stride, lead):
        left = value.shape[1]
        taken = 0
        while taken < left:
            t = (start + taken) // stride
            into = start + taken - t * stride
            count = min(left - taken, stride - into)
            right_own[p, t, :, lead + into : lead + into + count] = value[:, taken : taken + count]
            taken += count

    load_qkv.wait()
    load_out.wait()

    def project(rows_in, put):
        for part in range(3):
            weight = wqkv_ref[:, part * width : (part + 1) * width]
            put(part, dot(rows_in[:, 0:width], weight).astype(BF16))
        put(3, dot(rows_in[:, width : 2 * width], wout_ref[...], ((1,), (1,))).astype(BF16))

    def put_own(part, value):
        for p in range(parts):
            halo[p, 4, :, part * width : (part + 1) * width] = value[p * ROWS : (p + 1) * ROWS]

    project(xn[2].reshape(tokens, 2 * width), put_own)

    copy(0, 4).start()

    def relay(p):
        copy(p, 0).wait_recv()
        copy(p, 2).start()
        copy(p, 1).wait_recv()
        copy(p, 3).start()

    def project_others(p):
        copy(p, 2).wait_recv()
        copy(p, 3).wait_recv()

        @pl.when(p + 1 < parts)
        def _():
            copy(p + 1, 4).start()

        rows_in = jnp.concatenate([xn[1, p], xn[3, p], xn[0, p], xn[4, p]], axis=0)

        def put(part, value):
            for i, k in enumerate((2, 6, 0, 8)):
                halo[p, k, :, part * width : (part + 1) * width] = value[
                    i * ROWS : (i + 1) * ROWS
                ]

            for i in range(3):
                copy(p, 5 + 3 * part + i).start()

        project(rows_in, put)

    def attend(p):
        for k in range(4, COPIES):
            copy(p, k).wait_recv()
        rows = pl.ds(pl.multiple_of(p * ROWS, ROWS), ROWS)

        @pl.loop(0, pairs, unroll=pairs)
        def _(c):
            def load(k, part):
                return halo[p, k, :, columns(c, part)].astype(F32)

            query = load(4, 0)
            grad = halo[p, 4, :, columns(c, 3)]
            products = [split(query * load(k, 1)) for k in range(SPAN)]
            scores = dot(jnp.concatenate(products, axis=0), ones[...])
            products = [grad * halo[p, k, :, columns(c, 2)] for k in range(SPAN)]
            dots = dot(jnp.concatenate(products, axis=0), ones[0:WIDE])
            score = []
            for k in range(SPAN):
                g = f + (k - WINDOW)
                inside = (g >= 0) & (g < frames_all)
                inside = inside & (lax.div(g + clip, clip) == lax.div(f + clip, clip))
                cap = jnp.where(inside, 3e38, -1e30).astype(F32)
                score.append(jnp.minimum(scores[k * ROWS : (k + 1) * ROWS], cap))
            top = functools.reduce(jnp.maximum, score)
            raised = [jnp.exp(s - top) for s in score]
            scale = 1.0 / functools.reduce(jnp.add, raised)
            soft = [e * scale for e in raised]
            mixed = jnp.zeros((ROWS, WIDE), F32)
            centre = jnp.zeros((ROWS, WIDE), F32)
            weight_at = pl.ds(pl.multiple_of(c * 2 * WIDE, WIDE), WIDE)
            slope_at = pl.ds(pl.multiple_of(c * 2 * WIDE + WIDE, WIDE), WIDE)
            for k in range(SPAN):
                weight = soft[k].astype(BF16)
                wd[k, :, weight_at] = weight
                mixed += weight.astype(F32) * load(k, 2)
                centre += soft[k] * dots[k * ROWS : (k + 1) * ROWS]
            side = lax.div(c, pairs // CORES)
            mleft_own[side, p, :, columns(lax.rem(c, pairs // CORES), 0)] = mixed.astype(BF16)
            query_grad = jnp.zeros((ROWS, WIDE), F32)
            for k in range(SPAN):
                gap = dots[k * ROWS : (k + 1) * ROWS] - centre
                slope = (soft[k] * gap).astype(BF16)
                wd[k, :, slope_at] = slope
                query_grad += slope.astype(F32) * load(k, 1)
            dqkv_ref[rows, columns(c, 0)] = query_grad.astype(BF16)

        small = dot(wd[...].reshape(SPAN * ROWS, 2 * width), pick[...])
        for k in range(SPAN):
            packed = small[k * ROWS : k * ROWS + 16]
            for r in range(1, ROWS // 16):
                at_row = k * ROWS + r * 16
                packed += pltpu.roll(small[at_row : at_row + 16], 32 * r, 1)
            if k == WINDOW:
                rcomp[p, k] = packed.astype(BF16)
            else:
                comp[p, k] = packed.astype(BF16)
                comp_copy(p, k - WINDOW).start()

    def collect(p):
        for j in others:
            comp_copy(p, j).wait_recv()
        rows = pl.ds(pl.multiple_of(p * ROWS, ROWS), ROWS)
        for k in range(SPAN):
            packed = rcomp[p, k].astype(F32)
            for r in range(ROWS // 16):
                value = packed if r == 0 else pltpu.roll(packed, WIDE - 32 * r, 1)
                stack[k * ROWS + r * 16 : k * ROWS + (r + 1) * 16, :] = value.astype(BF16)

        @pl.loop(0, pairs, unroll=pairs)
        def _(c):
            wide = dot(stack[...], spill[:, columns(c, 0, 2 * WIDE)])
            key_grad = jnp.zeros((ROWS, WIDE), F32)
            value_grad = jnp.zeros((ROWS, WIDE), F32)
            for k in range(SPAN):
                piece = wide[k * ROWS : (k + 1) * ROWS]
                value_grad += piece[:, :WIDE] * halo[p, k, :, columns(c, 3)].astype(F32)
                key_grad += piece[:, WIDE:] * halo[p, k, :, columns(c, 0)].astype(F32)
            dqkv_ref[rows, columns(c, 1)] = key_grad.astype(BF16)
            dqkv_ref[rows, columns(c, 2)] = value_grad.astype(BF16)

        for m in range(3 * pairs):
            value = dqkv_ref[rows, m * WIDE : (m + 1) * WIDE]
            place(p, value, m * WIDE, share, 0)
        left_copy(p).start()
        right_copy(p).start()

    relay(0)
    start_own(2)
    for p in range(parts):
        for m in range(pairs):
            value = cot_ref[p * ROWS : (p + 1) * ROWS, m * WIDE : (m + 1) * WIDE]
            place(p, value, m * WIDE, width // tm_size, share)

    normed_copy.wait_recv()
    left_t[0, :, 0:tokens] = nleft_own[core].T
    left_t[0, :, tokens : 2 * tokens] = nleft_other[...].T

    relay(1)
    start_own(3)
    project_others(0)

    @pl.loop(0, parts)
    def _(p):
        @pl.when((p > 0) & (p + 2 < parts))
        def _():
            relay(p + 2)

        @pl.when((p > 0) & (p + 3 < parts))
        def _():
            start_own(p + 3)

        attend(p)

        @pl.when(p == 0)
        def _():
            relay(2)

        @pl.when(p + 1 < parts)
        def _():
            project_others(p + 1)

        @pl.when(p > 0)
        def _():
            collect(p - 1)

    collect(parts - 1)

    def f0_copy(yy, xh):
        return remote(
            f0_send.at[yy, xh],
            f0_recv.at[y, xh],
            f0_ssem.at[yy, xh],
            f0_rsem.at[y, xh],
            device(yy, x, z, core),
        )

    def f1_copy(yy, xh):
        return remote(
            f1_send.at[xh, yy],
            f1_recv.at[x, yy],
            f1_ssem.at[xh, yy],
            f1_rsem.at[x, yy],
            device(y, xh * X_LO + core, z, core),
        )

    for p in range(parts):
        left_copy(p).wait_recv()
    left_t[1, :, 0:tokens] = mleft_own[core].reshape(tokens, half_width).T
    left_t[1, :, tokens : 2 * tokens] = mleft_other[...].reshape(tokens, half_width).T
    for p in range(parts):
        right_copy(p).wait_recv()

    @pl.loop(0, tm_size)
    def _(i):
        t = turned(i + X_HI, y * X_HI, tm_size)
        yy, xh = lax.div(t, X_HI), lax.rem(t, X_HI)
        right = jnp.concatenate(
            [right_own[p, t] for p in range(parts)] + [right_other[p, t] for p in range(parts)],
            axis=0,
        )
        first = dot(left_t[0], right)
        last = (block - 1) // WIDE * WIDE
        second = dot(left_t[1], right[:, last:])
        lane = lax.broadcasted_iota(jnp.int32, second.shape, 1)
        tail = jnp.where(lane < share - last, first[:, last:], second)
        total[t, :, 0:last] = first[:, :last]
        total[t, :, last:block] = tail
        f0_send[yy, xh, :, 0:last] = first[:side_rows, :last].astype(BF16)
        f0_send[yy, xh, :, last:block] = tail[:side_rows].astype(BF16)
        f1_send[xh, yy, :, 0:last] = first[side_rows:, :last].astype(BF16)
        f1_send[xh, yy, :, last:block] = tail[side_rows:].astype(BF16)

        @pl.when(yy != y)
        def _():
            f0_copy(yy, xh).start()

        @pl.when(xh * X_LO + core != x)
        def _():
            f1_copy(yy, xh).start()

    normed_grad = dot(dqkv_ref[...], wqkv_ref[...], ((1,), (1,)))
    unit_rows = unit[...]
    gain_part = jnp.sum(normed_grad * unit_rows, axis=0, keepdims=True)
    gain_core[core] = jnp.zeros((8, WIDE), F32)
    for i in range(pairs):
        gain_core[core, i : i + 1, :] = gain_part[:, i * WIDE : (i + 1) * WIDE]

    def gain_exchange(buffer, own, count, spot, slot):
        return [
            remote(
                buffer.at[own],
                buffer.at[own],
                gain_ssem.at[slot, d],
                gain_rsem.at[slot, d],
                spot(turned(own, d, count)),
            )
            for d in range(1, count)
        ]

    def gain_sum(buffer, count):
        return functools.reduce(jnp.add, [buffer[i] for i in range(count)])

    core_gain = gain_exchange(gain_core, core, CORES, lambda cc: device(y, x, z, cc), 0)
    y_gain = gain_exchange(gain_y, y, ny, lambda yy: device(yy, x, z, core), 1)
    x_gain = gain_exchange(gain_x, x, nx, lambda xx: device(y, xx, z, core), 2)
    z_gain = gain_exchange(gain_z, z, nz, lambda zz: device(y, x, zz, core), 3)
    for move in core_gain:
        move.start()

    scaled = normed_grad * gain_ref[...].reshape(1, width)
    mean_one = jnp.mean(scaled, axis=-1, keepdims=True)
    second = jnp.mean(scaled * unit_rows, axis=-1, keepdims=True)
    back = spread[...] * (scaled - mean_one - unit_rows * second)
    fg_ref[...] = (cot_ref[...].astype(F32) + back).astype(BF16)
    mixed_out = x_ref[...].astype(F32)
    for i in range(CORES):
        mixed_half = mleft_own[i].reshape(tokens, half_width)
        mixed_out += dot(mixed_half, wout_ref[i * half_width : (i + 1) * half_width, :])
    bo_ref[...] = mixed_out.astype(BF16)

    for move in core_gain:
        move.wait_recv()
    gain_y[y] = gain_sum(gain_core, CORES)
    for move in y_gain:
        move.start()

    def n0_copy(xh):
        return remote(
            n0_send.at[xh],
            n0_recv.at[x],
            n0_ssem.at[xh],
            n0_rsem.at[x],
            device(y, xh * X_LO + core, z, core),
        )

    def n1_copy(yy):
        return remote(
            n1_send.at[yy],
            n1_recv.at[y],
            n1_ssem.at[yy],
            n1_rsem.at[y],
            device(yy, x, z, core),
        )

    def z_copy(zz):
        return remote(
            z_send.at[zz], z_recv.at[z], z_ssem.at[zz], z_rsem.at[z], device(y, x, zz, core)
        )

    def arrived(buffer, spot, sem):
        remote(buffer.at[spot], buffer.at[spot], sem.at[spot], sem.at[spot], partner).wait_recv()
        return buffer[spot].astype(F32)

    for step in range(1, X_HI + 1):
        xh = turned(x_hi, step, X_HI)
        value = total[y * X_HI + xh, 0:side_rows, :]
        for d in range(1, ny):
            value = value + arrived(f0_recv, (turned(y, d, ny), xh), f0_rsem)
        goal = xh * X_LO + core

        @pl.when(goal != x)
        def _():
            n0_send[xh] = value.astype(BF16)
            n0_copy(xh).start()

        @pl.when(goal == x)
        def _():
            n_total[0] = value

    @pl.when(active)
    def _():
        for step in range(1, ny + 1):
            yy = turned(y, step, ny)
            value = total[yy * X_HI + x_hi, side_rows : 2 * side_rows, :]
            for d in range(1, nx):
                value = value + arrived(f1_recv, (turned(x, d, nx), yy), f1_rsem)
            if step < ny:
                n1_send[yy] = value.astype(BF16)
                n1_copy(yy).start()
            else:
                n_total[1] = value

    for move in y_gain:
        move.wait_recv()
    gain_x[x] = gain_sum(gain_y, ny)
    for move in x_gain:
        move.start()

    @pl.when(active)
    def _():
        for side in range(2):
            value = n_total[side]
            for d in range(1, nx if side == 0 else ny):
                if side == 0:
                    value = value + arrived(n0_recv, turned(x, d, nx), n0_rsem)
                else:
                    value = value + arrived(n1_recv, turned(y, d, ny), n1_rsem)
            for i in range(nz // 2):
                zz = side * (nz // 2) + i
                piece = value[i * z_rows : (i + 1) * z_rows]
                z_total[zz] = piece
                z_send[zz] = piece.astype(BF16)

                @pl.when(zz != z)
                def _():
                    z_copy(zz).start()

    for move in x_gain:
        move.wait_recv()
    gain_z[z] = gain_sum(gain_x, nx)
    for move in z_gain:
        move.start()

    final = remote(final_send, final_recv, final_ssem, final_rsem, partner)

    def deliver(value):
        last = share // WIDE * WIDE
        wq_ref[:, 0:last] = value[:, :last]
        tail = value[:, last : last + WIDE]
        wq_ref[:, last:share] = tail[:, : share - last]
        if share == last:
            wo_ref[...] = tail
        else:
            count = block - share
            wo_ref[...] = pltpu.roll(tail, WIDE - (share - last), 1)[:, :count]

    @pl.when(active)
    def _():
        value = z_total[z]
        for d in range(1, nz):
            value = value + arrived(z_recv, turned(z, d, nz), z_rsem)
        value = value * inv_root
        lower = value[:final_rows]
        upper = value[final_rows:]
        final_send[...] = jnp.where(core == 0, upper, lower)
        final.start()
        deliver(jnp.where(core == 0, lower, upper))

    @pl.when(jnp.logical_not(active))
    def _():
        final.wait_recv()
        deliver(final_recv[...])

    for move in z_gain:
        move.wait_recv()
    gain_last[...] = gain_sum(gain_z, nz) * inv_root
    cut = width // inner
    row_one = lax.div(inner_at * cut, WIDE)
    lead = lax.rem(inner_at * cut, WIDE)
    low = jnp.broadcast_to(gain_last[pl.ds(row_one, 1), :], (8, WIDE))
    high = jnp.broadcast_to(gain_last[pl.ds(row_one + 1, 1), :], (8, WIDE))
    lane = lax.broadcasted_iota(jnp.int32, (8, WIDE), 1)
    shift = lax.rem(WIDE - lead, WIDE)
    merged = jnp.where(
        lane < WIDE - lead, pltpu.roll(low, shift, 1), pltpu.roll(high, shift, 1)
    )
    gout_ref[...] = merged[0:1, :cut]

    normed_copy.wait_send()
    for move in core_gain + y_gain + x_gain + z_gain:
        move.wait_send()

    @pl.loop(0, parts)
    def _(p):
        for k in range(COPIES):
            copy(p, k).wait_send()
        for j in others:
            comp_copy(p, j).wait_send()
        left_copy(p).wait_send()
        right_copy(p).wait_send()

    for xh in range(X_HI):
        for yy in range(ny):

            @pl.when(yy != y)
            def _():
                f0_copy(yy, xh).wait_send()

            @pl.when(xh * X_LO + core != x)
            def _():
                f1_copy(yy, xh).wait_send()

        @pl.when(xh * X_LO + core != x)
        def _():
            n0_copy(xh).wait_send()

    @pl.when(active)
    def _():
        for yy in range(ny):

            @pl.when(yy != y)
            def _():
                n1_copy(yy).wait_send()

        for zz in range(nz):

            @pl.when(zz != z)
            def _():
                z_copy(zz).wait_send()

        final.wait_send()


def copy_kernel(*refs):
    count = len(refs) // 2
    for source, target in zip(refs[:count], refs[count:], strict=True):
        target[...] = source[...].reshape(target.shape)


def hand_over(*arrays):
    vmem = pl.BlockSpec(memory_space=pltpu.VMEM)
    shapes = [a.shape for a in arrays[:-1]] + [(arrays[-1].size,)]
    return pl.pallas_call(
        copy_kernel,
        out_shape=tuple(
            jax.ShapeDtypeStruct(shape, a.dtype) for shape, a in zip(shapes, arrays, strict=True)
        ),
        in_specs=[vmem] * len(arrays),
        out_specs=(vmem,) * len(arrays),
        name="hand_over",
    )(*arrays)


def shards(frames, norm_gain, w_qkv, w_out, cotangent):
    tm_size, inner = lax.axis_size("tm"), lax.axis_size("inner")
    width = frames.shape[-1]
    tokens = frames.shape[0] * frames.shape[1]
    frames_all = tm_size * inner
    x = frames.reshape(tokens, width)
    cot = cotangent.reshape(tokens, width)
    ny, nx = tm_size // X_HI, X_HI * X_LO
    nz = inner // (X_LO * CORES)
    parts = tokens // ROWS
    half = width // CORES
    share = 3 * width // tm_size
    block = 4 * width // tm_size
    side = half // 2
    z_rows = half // nz
    final_rows = z_rows // CORES
    inv_root = 1.0 / math.sqrt(tokens * frames_all)
    sizes = (tm_size, inner, min(CLIP_MAX, frames_all), inv_root)
    vmem = pl.BlockSpec(memory_space=pltpu.VMEM)
    hbm = pl.BlockSpec(memory_space=pl.ANY)
    dma = pltpu.SemaphoreType.DMA
    block_out, frames_grad, qkv_share, out_share, gain_sum = pl.pallas_call(
        functools.partial(block_kernel, sizes),
        out_shape=(
            jax.ShapeDtypeStruct((tokens, width), BF16),
            jax.ShapeDtypeStruct((tokens, width), BF16),
            jax.ShapeDtypeStruct((final_rows, share), F32),
            jax.ShapeDtypeStruct((final_rows, block - share), F32),
            jax.ShapeDtypeStruct((1, width // inner), F32),
        ),
        in_specs=[vmem, vmem, vmem, hbm, hbm],
        out_specs=(vmem,) * 5,
        scratch_shapes=[
            pltpu.VMEM(w_qkv.shape, BF16),
            pltpu.VMEM(w_out.shape, BF16),
            pltpu.VMEM((5, parts, ROWS, 2 * width), BF16),
            pltpu.VMEM((parts, SPAN, ROWS, 4 * width), BF16),
            pltpu.VMEM((parts, SPAN, 16, WIDE), BF16),
            pltpu.VMEM((parts, SPAN, 16, WIDE), BF16),
            pltpu.VMEM((SPAN, ROWS, 2 * width), BF16),
            pltpu.VMEM((SPAN * ROWS, WIDE), BF16),
            pltpu.VMEM((tokens, 3 * width), BF16),
            pltpu.VMEM((tokens, width), F32),
            pltpu.VMEM((tokens, 1), F32),
            pltpu.VMEM((2 * WIDE, WIDE), BF16),
            pltpu.VMEM((2 * width, WIDE), BF16),
            pltpu.VMEM((WIDE, 2 * width), BF16),
            pltpu.VMEM((parts, tm_size, ROWS, block), BF16),
            pltpu.VMEM((parts, tm_size, ROWS, block), BF16),
            pltpu.VMEM((CORES, tokens, half), BF16),
            pltpu.VMEM((tokens, half), BF16),
            pltpu.VMEM((CORES, parts, ROWS, half), BF16),
            pltpu.VMEM((parts, ROWS, half), BF16),
            pltpu.VMEM((2, half, 2 * tokens), BF16),
            pltpu.VMEM((tm_size, half, block), F32),
            pltpu.VMEM((ny, X_HI, side, block), BF16),
            pltpu.VMEM((ny, X_HI, side, block), BF16),
            pltpu.VMEM((X_HI, ny, side, block), BF16),
            pltpu.VMEM((nx, ny, side, block), BF16),
            pltpu.VMEM((2, side, block), F32),
            pltpu.VMEM((X_HI, side, block), BF16),
            pltpu.VMEM((nx, side, block), BF16),
            pltpu.VMEM((ny, side, block), BF16),
            pltpu.VMEM((ny, side, block), BF16),
            pltpu.VMEM((nz, z_rows, block), F32),
            pltpu.VMEM((nz, z_rows, block), BF16),
            pltpu.VMEM((nz, z_rows, block), BF16),
            pltpu.VMEM((final_rows, block), F32),
            pltpu.VMEM((final_rows, block), F32),
            pltpu.VMEM((CORES, 8, WIDE), F32),
            pltpu.VMEM((ny, 8, WIDE), F32),
            pltpu.VMEM((nx, 8, WIDE), F32),
            pltpu.VMEM((nz, 8, WIDE), F32),
            pltpu.VMEM((8, WIDE), F32),
            dma((2,)),
            dma((parts, COPIES)),
            dma((parts, COPIES)),
            dma((parts, SPAN)),
            dma((parts, SPAN)),
            dma((parts, 3)),
            dma((parts, 3)),
            dma((ny, X_HI)),
            dma((ny, X_HI)),
            dma((X_HI, ny)),
            dma((nx, ny)),
            dma((X_HI,)),
            dma((nx,)),
            dma((ny,)),
            dma((ny,)),
            dma((nz,)),
            dma((nz,)),
            dma,
            dma,
            dma((4, nz)),
            dma((4, nz)),
        ],
        compiler_params=pltpu.CompilerParams(
            collective_id=0, has_side_effects=True, vmem_limit_bytes=60 * 2**20
        ),
        name="attention_block",
    )(x, norm_gain, cot, w_qkv, w_out)
    outs = hand_over(block_out, frames_grad, qkv_share, out_share, gain_sum)
    return (
        outs[0].reshape(frames.shape),
        outs[1].reshape(frames.shape),
        outs[2],
        outs[3],
        outs[4],
    )


def solution(mesh):
    in_specs = (P(("tm", "inner"), None, None), P(), P(), P(), P(("tm", "inner"), None, None))
    out_specs = (
        P(("tm", "inner"), None, None),
        P(("tm", "inner"), None, None),
        P("inner", "tm"),
        P("inner", "tm"),
        P("inner"),
    )
    return jax.shard_map(shards, mesh=mesh, in_specs=in_specs, out_specs=out_specs, check_vma=False)
```

```python
import functools
import math

import jax
import jax.numpy as jnp
from jax import lax
from jax.experimental import pallas as pl
from jax.experimental.pallas import tpu as pltpu
from jax.sharding import PartitionSpec as P

HEAD_DIM = 64
WINDOW = 4
CLIP_MAX = 256
EPSILON = 1e-06
SPAN = 2 * WINDOW + 1
WIDE = 128
ROWS = 64
COPIES = 21
CORES = 2
X_LO = 2
X_HI = 2
MESH = pl.DeviceIdType.MESH
F32 = jnp.float32
BF16 = jnp.bfloat16


def dot(a, b, dims=((1,), (0,))):
    return lax.dot_general(a, b, (dims, ((), ())), preferred_element_type=F32)


def split(wide_vals):
    high = wide_vals.astype(BF16)
    low = (wide_vals - high.astype(F32)).astype(BF16)
    return jnp.concatenate([high, low], axis=1)


def remote(source, target, ssem, rsem, where):
    return pltpu.make_async_remote_copy(
        src_ref=source,
        dst_ref=target,
        send_sem=ssem,
        recv_sem=rsem,
        device_id=where,
        device_id_type=MESH,
    )


def turned(value, step, count):
    return lax.rem(value + step, count)


def block_kernel(
    sizes,
    x_ref,
    gain_ref,
    cot_ref,
    wqkv_hbm,
    wout_hbm,
    bo_ref,
    fg_ref,
    wq_ref,
    wo_ref,
    gout_ref,
    wqkv_ref,
    wout_ref,
    xn,
    halo,
    comp,
    rcomp,
    wd,
    stack,
    dqkv_ref,
    unit,
    spread,
    ones,
    pick,
    spill,
    right_own,
    right_other,
    nleft_own,
    nleft_other,
    mleft_own,
    mleft_other,
    left_t,
    total,
    f0_send,
    f0_recv,
    f1_send,
    f1_recv,
    n_total,
    n0_send,
    n0_recv,
    n1_send,
    n1_recv,
    z_total,
    z_send,
    z_recv,
    final_send,
    final_recv,
    gain_core,
    gain_y,
    gain_x,
    gain_z,
    gain_last,
    load_sem,
    send_sem,
    recv_sem,
    csend_sem,
    crecv_sem,
    gsend_sem,
    grecv_sem,
    f0_ssem,
    f0_rsem,
    f1_ssem,
    f1_rsem,
    n0_ssem,
    n0_rsem,
    n1_ssem,
    n1_rsem,
    z_ssem,
    z_rsem,
    final_ssem,
    final_rsem,
    gain_ssem,
    gain_rsem,
):
    tm_size, inner, clip, inv_root = sizes
    frames_all = tm_size * inner
    tokens, width = x_ref.shape
    pairs = width // WIDE
    parts = tokens // ROWS
    ny, nx = tm_size // X_HI, X_HI * X_LO
    nz = inner // (X_LO * CORES)
    half_width = width // CORES
    share = 3 * width // tm_size
    block = 4 * width // tm_size
    side_rows = half_width // 2
    z_rows = half_width // nz
    final_rows = z_rows // CORES

    tm_at = lax.axis_index("tm")
    inner_at = lax.axis_index("inner")
    f = tm_at * inner + inner_at
    odd = lax.rem(f, 2)
    core = lax.rem(inner_at, CORES)
    z = lax.rem(lax.div(inner_at, CORES), nz)
    x_lo = lax.div(inner_at, CORES * nz)
    x_hi = lax.rem(tm_at, X_HI)
    x = x_hi * X_LO + x_lo
    y = lax.div(tm_at, X_HI)
    active = x_lo == core

    def at(offset):
        g = lax.rem(f + offset + frames_all, frames_all)
        return (lax.div(g, inner), lax.rem(g, inner))

    def device(yy, xx, zz, cc):
        return (
            yy * X_HI + lax.div(xx, X_LO),
            (lax.rem(xx, X_LO) * nz + zz) * CORES + cc,
        )

    partner = device(y, x, z, 1 - core)
    others = [j for j in range(-WINDOW, WINDOW + 1) if j != 0]
    peers = [at(j) for j in others]
    peers += [device(turned(y, d, ny), x, z, core) for d in range(1, ny)]
    peers += [device(y, turned(x, d, nx), z, core) for d in range(1, nx)]
    peers += [device(y, x, turned(z, d, nz), core) for d in range(1, nz)]
    barrier = pltpu.get_barrier_semaphore()
    for peer in peers:
        pl.semaphore_signal(barrier, inc=1, device_id=peer, device_id_type=MESH)

    load_qkv = pltpu.make_async_copy(wqkv_hbm, wqkv_ref, load_sem.at[0])
    load_out = pltpu.make_async_copy(wout_hbm, wout_ref, load_sem.at[1])
    load_qkv.start()
    load_out.start()

    def normalize(p):
        rows = slice(p * ROWS, (p + 1) * ROWS)
        wide_vals = x_ref[rows, :].astype(F32)
        center = wide_vals - jnp.mean(wide_vals, axis=-1, keepdims=True)
        variance = jnp.mean(center * center, axis=-1, keepdims=True)
        spread_one = lax.rsqrt(variance + EPSILON)
        unit_rows = center * spread_one
        unit[rows, :] = unit_rows
        spread[rows, :] = spread_one
        normed = (unit_rows * gain_ref[...].reshape(1, width)).astype(BF16)
        xn[2, p, :, 0:width] = normed
        xn[2, p, :, width : 2 * width] = cot_ref[rows, :]
        for i in range(CORES):
            nleft_own[i, rows, :] = normed[:, i * half_width : (i + 1) * half_width]

    normalize(0)

    def columns(c, part, size=WIDE):
        return pl.ds(pl.multiple_of(part * width + c * size, size), size)

    def copy(p, k):
        if k < 8:
            way = k // 2
            rows = pl.ds(k % 2 * (ROWS // 2), ROWS // 2)
            source = xn.at[(2, 2, 1, 3)[way], p, rows]
            target = xn.at[(1, 3, 0, 4)[way], p, rows]
            where = at((2, -2, 2, -2)[way])
        elif k == 8:
            source = halo.at[p, 4]
            target = halo.at[p, 3 + 2 * odd]
            where = partner
        else:
            slot = (2, 6, 8 - 8 * odd)[(k - 9) % 3]
            part = (k - 9) // 3
            lanes = pl.ds(part * width, width)
            source = halo.at[p, slot, :, lanes]
            target = halo.at[p, slot - 1 + 2 * odd, :, lanes]
            where = partner
        return remote(source, target, send_sem.at[p, k], recv_sem.at[p, k], where)

    def comp_copy(p, j):
        k = j + WINDOW
        return remote(
            comp.at[p, k],
            rcomp.at[p, SPAN - 1 - k],
            csend_sem.at[p, k],
            crecv_sem.at[p, k],
            at(j),
        )

    normed_copy = remote(
        nleft_own.at[1 - core], nleft_other, gsend_sem.at[0, 2], grecv_sem.at[0, 2], partner
    )

    def left_copy(p):
        return remote(
            mleft_own.at[1 - core, p],
            mleft_other.at[p],
            gsend_sem.at[p, 0],
            grecv_sem.at[p, 0],
            partner,
        )

    def right_copy(p):
        return remote(
            right_own.at[p], right_other.at[p], gsend_sem.at[p, 1], grecv_sem.at[p, 1], partner
        )

    pl.semaphore_wait(barrier, len(peers))

    def start_own(p):
        for k in (0, 2, 1, 3):
            copy(p, k).start()

    def relay_half(p, half):
        for way in range(2):
            copy(p, 2 * way + half).wait_recv()
            copy(p, 4 + 2 * way + half).start()

    def relay(p):
        relay_half(p, 0)
        relay_half(p, 1)

    start_own(0)
    for p in range(1, parts):
        normalize(p)
    normed_copy.start()

    row_at = lax.broadcasted_iota(jnp.int32, (2 * WIDE, WIDE), 0)
    lane_at = lax.broadcasted_iota(jnp.int32, (2 * WIDE, WIDE), 1)
    same = (lax.rem(row_at, WIDE) // HEAD_DIM) == (lane_at // HEAD_DIM)
    ones[...] = jnp.where(same, HEAD_DIM**-0.5, 0.0).astype(BF16)
    row_at = lax.broadcasted_iota(jnp.int32, pick.shape, 0)
    lane_at = lax.broadcasted_iota(jnp.int32, pick.shape, 1)
    pick[...] = jnp.where(row_at == lane_at * HEAD_DIM, 1.0, 0.0).astype(BF16)
    row_at = lax.broadcasted_iota(jnp.int32, spill.shape, 0)
    lane_at = lax.broadcasted_iota(jnp.int32, spill.shape, 1)
    spill[...] = jnp.where(lane_at // HEAD_DIM == row_at, 1.0, 0.0).astype(BF16)

    def place(p, value, start, stride, lead):
        left = value.shape[1]
        taken = 0
        while taken < left:
            t = (start + taken) // stride
            into = start + taken - t * stride
            count = min(left - taken, stride - into)
            right_own[p, t, :, lead + into : lead + into + count] = value[:, taken : taken + count]
            taken += count

    relay_half(0, 0)
    start_own(1)
    load_qkv.wait()
    load_out.wait()

    def project(rows_in, put):
        for part in range(3):
            weight = wqkv_ref[:, part * width : (part + 1) * width]
            put(part, dot(rows_in[:, 0:width], weight).astype(BF16))
        put(3, dot(rows_in[:, width : 2 * width], wout_ref[...], ((1,), (1,))).astype(BF16))

    def put_own(part, value):
        for p in range(parts):
            halo[p, 4, :, part * width : (part + 1) * width] = value[p * ROWS : (p + 1) * ROWS]

    project(xn[2].reshape(tokens, 2 * width), put_own)

    copy(0, 8).start()

    def project_others(p):
        for k in range(4, 8):
            copy(p, k).wait_recv()

        @pl.when(p + 1 < parts)
        def _():
            copy(p + 1, 8).start()

        rows_in = jnp.concatenate([xn[1, p], xn[3, p], xn[0, p], xn[4, p]], axis=0)

        def put(part, value):
            for i, k in enumerate((2, 6, 0, 8)):
                halo[p, k, :, part * width : (part + 1) * width] = value[
                    i * ROWS : (i + 1) * ROWS
                ]

            for i in range(3):
                copy(p, 9 + 3 * part + i).start()

        project(rows_in, put)

    def attend(p):
        for k in range(8, COPIES):
            copy(p, k).wait_recv()
        rows = pl.ds(pl.multiple_of(p * ROWS, ROWS), ROWS)

        @pl.loop(0, pairs, unroll=pairs)
        def _(c):
            def load(k, part):
                return halo[p, k, :, columns(c, part)].astype(F32)

            query = load(4, 0)
            grad = halo[p, 4, :, columns(c, 3)]
            products = [split(query * load(k, 1)) for k in range(SPAN)]
            scores = dot(jnp.concatenate(products, axis=0), ones[...])
            products = [grad * halo[p, k, :, columns(c, 2)] for k in range(SPAN)]
            dots = dot(jnp.concatenate(products, axis=0), ones[0:WIDE])
            score = []
            for k in range(SPAN):
                g = f + (k - WINDOW)
                inside = (g >= 0) & (g < frames_all)
                inside = inside & (lax.div(g + clip, clip) == lax.div(f + clip, clip))
                cap = jnp.where(inside, 3e38, -1e30).astype(F32)
                score.append(jnp.minimum(scores[k * ROWS : (k + 1) * ROWS], cap))
            top = functools.reduce(jnp.maximum, score)
            raised = [jnp.exp(s - top) for s in score]
            scale = 1.0 / functools.reduce(jnp.add, raised)
            soft = [e * scale for e in raised]
            mixed = jnp.zeros((ROWS, WIDE), F32)
            centre = jnp.zeros((ROWS, WIDE), F32)
            weight_at = pl.ds(pl.multiple_of(c * 2 * WIDE, WIDE), WIDE)
            slope_at = pl.ds(pl.multiple_of(c * 2 * WIDE + WIDE, WIDE), WIDE)
            for k in range(SPAN):
                weight = soft[k].astype(BF16)
                wd[k, :, weight_at] = weight
                mixed += weight.astype(F32) * load(k, 2)
                centre += soft[k] * dots[k * ROWS : (k + 1) * ROWS]
            side = lax.div(c, pairs // CORES)
            mleft_own[side, p, :, columns(lax.rem(c, pairs // CORES), 0)] = mixed.astype(BF16)
            query_grad = jnp.zeros((ROWS, WIDE), F32)
            for k in range(SPAN):
                gap = dots[k * ROWS : (k + 1) * ROWS] - centre
                slope = (soft[k] * gap).astype(BF16)
                wd[k, :, slope_at] = slope
                query_grad += slope.astype(F32) * load(k, 1)
            dqkv_ref[rows, columns(c, 0)] = query_grad.astype(BF16)

        small = dot(wd[...].reshape(SPAN * ROWS, 2 * width), pick[...])
        for k in range(SPAN):
            packed = small[k * ROWS : k * ROWS + 16]
            for r in range(1, ROWS // 16):
                at_row = k * ROWS + r * 16
                packed += pltpu.roll(small[at_row : at_row + 16], 32 * r, 1)
            if k == WINDOW:
                rcomp[p, k] = packed.astype(BF16)
            else:
                comp[p, k] = packed.astype(BF16)
                comp_copy(p, k - WINDOW).start()

    def collect(p):
        for j in others:
            comp_copy(p, j).wait_recv()
        rows = pl.ds(pl.multiple_of(p * ROWS, ROWS), ROWS)
        for k in range(SPAN):
            packed = rcomp[p, k].astype(F32)
            for r in range(ROWS // 16):
                value = packed if r == 0 else pltpu.roll(packed, WIDE - 32 * r, 1)
                stack[k * ROWS + r * 16 : k * ROWS + (r + 1) * 16, :] = value.astype(BF16)

        @pl.loop(0, pairs, unroll=pairs)
        def _(c):
            wide = dot(stack[...], spill[:, columns(c, 0, 2 * WIDE)])
            key_grad = jnp.zeros((ROWS, WIDE), F32)
            value_grad = jnp.zeros((ROWS, WIDE), F32)
            for k in range(SPAN):
                piece = wide[k * ROWS : (k + 1) * ROWS]
                value_grad += piece[:, :WIDE] * halo[p, k, :, columns(c, 3)].astype(F32)
                key_grad += piece[:, WIDE:] * halo[p, k, :, columns(c, 0)].astype(F32)
            dqkv_ref[rows, columns(c, 1)] = key_grad.astype(BF16)
            dqkv_ref[rows, columns(c, 2)] = value_grad.astype(BF16)

        for m in range(3 * pairs):
            value = dqkv_ref[rows, m * WIDE : (m + 1) * WIDE]
            place(p, value, m * WIDE, share, 0)
        left_copy(p).start()
        right_copy(p).start()

    relay_half(0, 1)
    start_own(2)
    for p in range(parts):
        for m in range(pairs):
            value = cot_ref[p * ROWS : (p + 1) * ROWS, m * WIDE : (m + 1) * WIDE]
            place(p, value, m * WIDE, width // tm_size, share)

    normed_copy.wait_recv()
    left_t[0, :, 0:tokens] = nleft_own[core].T
    left_t[0, :, tokens : 2 * tokens] = nleft_other[...].T

    relay(1)
    start_own(3)
    project_others(0)

    @pl.loop(0, parts)
    def _(p):
        @pl.when((p > 0) & (p + 2 < parts))
        def _():
            relay(p + 2)

        @pl.when((p > 0) & (p + 3 < parts))
        def _():
            start_own(p + 3)

        attend(p)

        @pl.when(p == 0)
        def _():
            relay(2)

        @pl.when(p + 1 < parts)
        def _():
            project_others(p + 1)

        @pl.when(p > 0)
        def _():
            collect(p - 1)

    collect(parts - 1)

    def f0_copy(yy, xh):
        return remote(
            f0_send.at[yy, xh],
            f0_recv.at[y, xh],
            f0_ssem.at[yy, xh],
            f0_rsem.at[y, xh],
            device(yy, x, z, core),
        )

    def f1_copy(yy, xh):
        return remote(
            f1_send.at[xh, yy],
            f1_recv.at[x, yy],
            f1_ssem.at[xh, yy],
            f1_rsem.at[x, yy],
            device(y, xh * X_LO + core, z, core),
        )

    for p in range(parts):
        left_copy(p).wait_recv()
    left_t[1, :, 0:tokens] = mleft_own[core].reshape(tokens, half_width).T
    left_t[1, :, tokens : 2 * tokens] = mleft_other[...].reshape(tokens, half_width).T
    for p in range(parts):
        right_copy(p).wait_recv()

    @pl.loop(0, tm_size)
    def _(i):
        t = turned(i + X_HI, y * X_HI, tm_size)
        yy, xh = lax.div(t, X_HI), lax.rem(t, X_HI)
        right = jnp.concatenate(
            [right_own[p, t] for p in range(parts)] + [right_other[p, t] for p in range(parts)],
            axis=0,
        )
        first = dot(left_t[0], right)
        last = (block - 1) // WIDE * WIDE
        second = dot(left_t[1], right[:, last:])
        lane = lax.broadcasted_iota(jnp.int32, second.shape, 1)
        tail = jnp.where(lane < share - last, first[:, last:], second)
        total[t, :, 0:last] = first[:, :last]
        total[t, :, last:block] = tail
        f0_send[yy, xh, :, 0:last] = first[:side_rows, :last].astype(BF16)
        f0_send[yy, xh, :, last:block] = tail[:side_rows].astype(BF16)
        f1_send[xh, yy, :, 0:last] = first[side_rows:, :last].astype(BF16)
        f1_send[xh, yy, :, last:block] = tail[side_rows:].astype(BF16)

        @pl.when(yy != y)
        def _():
            f0_copy(yy, xh).start()

        @pl.when(xh * X_LO + core != x)
        def _():
            f1_copy(yy, xh).start()

    normed_grad = dot(dqkv_ref[...], wqkv_ref[...], ((1,), (1,)))
    unit_rows = unit[...]
    gain_part = jnp.sum(normed_grad * unit_rows, axis=0, keepdims=True)
    gain_core[core] = jnp.zeros((8, WIDE), F32)
    for i in range(pairs):
        gain_core[core, i : i + 1, :] = gain_part[:, i * WIDE : (i + 1) * WIDE]

    def gain_exchange(buffer, own, count, spot, slot):
        return [
            remote(
                buffer.at[own],
                buffer.at[own],
                gain_ssem.at[slot, d],
                gain_rsem.at[slot, d],
                spot(turned(own, d, count)),
            )
            for d in range(1, count)
        ]

    def gain_sum(buffer, count):
        return functools.reduce(jnp.add, [buffer[i] for i in range(count)])

    core_gain = gain_exchange(gain_core, core, CORES, lambda cc: device(y, x, z, cc), 0)
    y_gain = gain_exchange(gain_y, y, ny, lambda yy: device(yy, x, z, core), 1)
    x_gain = gain_exchange(gain_x, x, nx, lambda xx: device(y, xx, z, core), 2)
    z_gain = gain_exchange(gain_z, z, nz, lambda zz: device(y, x, zz, core), 3)
    for move in core_gain:
        move.start()

    scaled = normed_grad * gain_ref[...].reshape(1, width)
    mean_one = jnp.mean(scaled, axis=-1, keepdims=True)
    second = jnp.mean(scaled * unit_rows, axis=-1, keepdims=True)
    back = spread[...] * (scaled - mean_one - unit_rows * second)
    fg_ref[...] = (cot_ref[...].astype(F32) + back).astype(BF16)
    mixed_out = x_ref[...].astype(F32)
    for i in range(CORES):
        mixed_half = mleft_own[i].reshape(tokens, half_width)
        mixed_out += dot(mixed_half, wout_ref[i * half_width : (i + 1) * half_width, :])
    bo_ref[...] = mixed_out.astype(BF16)

    for move in core_gain:
        move.wait_recv()
    gain_y[y] = gain_sum(gain_core, CORES)
    for move in y_gain:
        move.start()

    def n0_copy(xh):
        return remote(
            n0_send.at[xh],
            n0_recv.at[x],
            n0_ssem.at[xh],
            n0_rsem.at[x],
            device(y, xh * X_LO + core, z, core),
        )

    def n1_copy(yy):
        return remote(
            n1_send.at[yy],
            n1_recv.at[y],
            n1_ssem.at[yy],
            n1_rsem.at[y],
            device(yy, x, z, core),
        )

    def z_copy(zz):
        return remote(
            z_send.at[zz], z_recv.at[z], z_ssem.at[zz], z_rsem.at[z], device(y, x, zz, core)
        )

    def arrived(buffer, spot, sem):
        remote(buffer.at[spot], buffer.at[spot], sem.at[spot], sem.at[spot], partner).wait_recv()
        return buffer[spot].astype(F32)

    for step in range(1, X_HI + 1):
        xh = turned(x_hi, step, X_HI)
        value = total[y * X_HI + xh, 0:side_rows, :]
        for d in range(1, ny):
            value = value + arrived(f0_recv, (turned(y, d, ny), xh), f0_rsem)
        goal = xh * X_LO + core

        @pl.when(goal != x)
        def _():
            n0_send[xh] = value.astype(BF16)
            n0_copy(xh).start()

        @pl.when(goal == x)
        def _():
            n_total[0] = value

    @pl.when(active)
    def _():
        for step in range(1, ny + 1):
            yy = turned(y, step, ny)
            value = total[yy * X_HI + x_hi, side_rows : 2 * side_rows, :]
            for d in range(1, nx):
                value = value + arrived(f1_recv, (turned(x, d, nx), yy), f1_rsem)
            if step < ny:
                n1_send[yy] = value.astype(BF16)
                n1_copy(yy).start()
            else:
                n_total[1] = value

    for move in y_gain:
        move.wait_recv()
    gain_x[x] = gain_sum(gain_y, ny)
    for move in x_gain:
        move.start()

    @pl.when(active)
    def _():
        for side in range(2):
            value = n_total[side]
            for d in range(1, nx if side == 0 else ny):
                if side == 0:
                    value = value + arrived(n0_recv, turned(x, d, nx), n0_rsem)
                else:
                    value = value + arrived(n1_recv, turned(y, d, ny), n1_rsem)
            for i in range(nz // 2):
                zz = side * (nz // 2) + i
                piece = value[i * z_rows : (i + 1) * z_rows]
                z_total[zz] = piece
                z_send[zz] = piece.astype(BF16)

                @pl.when(zz != z)
                def _():
                    z_copy(zz).start()

    for move in x_gain:
        move.wait_recv()
    gain_z[z] = gain_sum(gain_x, nx)
    for move in z_gain:
        move.start()

    final = remote(final_send, final_recv, final_ssem, final_rsem, partner)

    def deliver(value):
        last = share // WIDE * WIDE
        wq_ref[:, 0:last] = value[:, :last]
        tail = value[:, last : last + WIDE]
        wq_ref[:, last:share] = tail[:, : share - last]
        if share == last:
            wo_ref[...] = tail
        else:
            count = block - share
            wo_ref[...] = pltpu.roll(tail, WIDE - (share - last), 1)[:, :count]

    @pl.when(active)
    def _():
        value = z_total[z]
        for d in range(1, nz):
            value = value + arrived(z_recv, turned(z, d, nz), z_rsem)
        value = value * inv_root
        lower = value[:final_rows]
        upper = value[final_rows:]
        final_send[...] = jnp.where(core == 0, upper, lower)
        final.start()
        deliver(jnp.where(core == 0, lower, upper))

    @pl.when(jnp.logical_not(active))
    def _():
        final.wait_recv()
        deliver(final_recv[...])

    for move in z_gain:
        move.wait_recv()
    gain_last[...] = gain_sum(gain_z, nz) * inv_root
    cut = width // inner
    row_one = lax.div(inner_at * cut, WIDE)
    lead = lax.rem(inner_at * cut, WIDE)
    low = jnp.broadcast_to(gain_last[pl.ds(row_one, 1), :], (8, WIDE))
    high = jnp.broadcast_to(gain_last[pl.ds(row_one + 1, 1), :], (8, WIDE))
    lane = lax.broadcasted_iota(jnp.int32, (8, WIDE), 1)
    shift = lax.rem(WIDE - lead, WIDE)
    merged = jnp.where(
        lane < WIDE - lead, pltpu.roll(low, shift, 1), pltpu.roll(high, shift, 1)
    )
    gout_ref[...] = merged[0:1, :cut]

    normed_copy.wait_send()
    for move in core_gain + y_gain + x_gain + z_gain:
        move.wait_send()

    @pl.loop(0, parts)
    def _(p):
        for k in range(COPIES):
            copy(p, k).wait_send()
        for j in others:
            comp_copy(p, j).wait_send()
        left_copy(p).wait_send()
        right_copy(p).wait_send()

    for xh in range(X_HI):
        for yy in range(ny):

            @pl.when(yy != y)
            def _():
                f0_copy(yy, xh).wait_send()

            @pl.when(xh * X_LO + core != x)
            def _():
                f1_copy(yy, xh).wait_send()

        @pl.when(xh * X_LO + core != x)
        def _():
            n0_copy(xh).wait_send()

    @pl.when(active)
    def _():
        for yy in range(ny):

            @pl.when(yy != y)
            def _():
                n1_copy(yy).wait_send()

        for zz in range(nz):

            @pl.when(zz != z)
            def _():
                z_copy(zz).wait_send()

        final.wait_send()


def copy_kernel(*refs):
    count = len(refs) // 2
    for source, target in zip(refs[:count], refs[count:], strict=True):
        target[...] = source[...].reshape(target.shape)


def hand_over(*arrays):
    vmem = pl.BlockSpec(memory_space=pltpu.VMEM)
    shapes = [a.shape for a in arrays[:-1]] + [(arrays[-1].size,)]
    return pl.pallas_call(
        copy_kernel,
        out_shape=tuple(
            jax.ShapeDtypeStruct(shape, a.dtype) for shape, a in zip(shapes, arrays, strict=True)
        ),
        in_specs=[vmem] * len(arrays),
        out_specs=(vmem,) * len(arrays),
        name="hand_over",
    )(*arrays)


def shards(frames, norm_gain, w_qkv, w_out, cotangent):
    tm_size, inner = lax.axis_size("tm"), lax.axis_size("inner")
    width = frames.shape[-1]
    tokens = frames.shape[0] * frames.shape[1]
    frames_all = tm_size * inner
    x = frames.reshape(tokens, width)
    cot = cotangent.reshape(tokens, width)
    ny, nx = tm_size // X_HI, X_HI * X_LO
    nz = inner // (X_LO * CORES)
    parts = tokens // ROWS
    half = width // CORES
    share = 3 * width // tm_size
    block = 4 * width // tm_size
    side = half // 2
    z_rows = half // nz
    final_rows = z_rows // CORES
    inv_root = 1.0 / math.sqrt(tokens * frames_all)
    sizes = (tm_size, inner, min(CLIP_MAX, frames_all), inv_root)
    vmem = pl.BlockSpec(memory_space=pltpu.VMEM)
    hbm = pl.BlockSpec(memory_space=pl.ANY)
    dma = pltpu.SemaphoreType.DMA
    block_out, frames_grad, qkv_share, out_share, gain_sum = pl.pallas_call(
        functools.partial(block_kernel, sizes),
        out_shape=(
            jax.ShapeDtypeStruct((tokens, width), BF16),
            jax.ShapeDtypeStruct((tokens, width), BF16),
            jax.ShapeDtypeStruct((final_rows, share), F32),
            jax.ShapeDtypeStruct((final_rows, block - share), F32),
            jax.ShapeDtypeStruct((1, width // inner), F32),
        ),
        in_specs=[vmem, vmem, vmem, hbm, hbm],
        out_specs=(vmem,) * 5,
        scratch_shapes=[
            pltpu.VMEM(w_qkv.shape, BF16),
            pltpu.VMEM(w_out.shape, BF16),
            pltpu.VMEM((5, parts, ROWS, 2 * width), BF16),
            pltpu.VMEM((parts, SPAN, ROWS, 4 * width), BF16),
            pltpu.VMEM((parts, SPAN, 16, WIDE), BF16),
            pltpu.VMEM((parts, SPAN, 16, WIDE), BF16),
            pltpu.VMEM((SPAN, ROWS, 2 * width), BF16),
            pltpu.VMEM((SPAN * ROWS, WIDE), BF16),
            pltpu.VMEM((tokens, 3 * width), BF16),
            pltpu.VMEM((tokens, width), F32),
            pltpu.VMEM((tokens, 1), F32),
            pltpu.VMEM((2 * WIDE, WIDE), BF16),
            pltpu.VMEM((2 * width, WIDE), BF16),
            pltpu.VMEM((WIDE, 2 * width), BF16),
            pltpu.VMEM((parts, tm_size, ROWS, block), BF16),
            pltpu.VMEM((parts, tm_size, ROWS, block), BF16),
            pltpu.VMEM((CORES, tokens, half), BF16),
            pltpu.VMEM((tokens, half), BF16),
            pltpu.VMEM((CORES, parts, ROWS, half), BF16),
            pltpu.VMEM((parts, ROWS, half), BF16),
            pltpu.VMEM((2, half, 2 * tokens), BF16),
            pltpu.VMEM((tm_size, half, block), F32),
            pltpu.VMEM((ny, X_HI, side, block), BF16),
            pltpu.VMEM((ny, X_HI, side, block), BF16),
            pltpu.VMEM((X_HI, ny, side, block), BF16),
            pltpu.VMEM((nx, ny, side, block), BF16),
            pltpu.VMEM((2, side, block), F32),
            pltpu.VMEM((X_HI, side, block), BF16),
            pltpu.VMEM((nx, side, block), BF16),
            pltpu.VMEM((ny, side, block), BF16),
            pltpu.VMEM((ny, side, block), BF16),
            pltpu.VMEM((nz, z_rows, block), F32),
            pltpu.VMEM((nz, z_rows, block), BF16),
            pltpu.VMEM((nz, z_rows, block), BF16),
            pltpu.VMEM((final_rows, block), F32),
            pltpu.VMEM((final_rows, block), F32),
            pltpu.VMEM((CORES, 8, WIDE), F32),
            pltpu.VMEM((ny, 8, WIDE), F32),
            pltpu.VMEM((nx, 8, WIDE), F32),
            pltpu.VMEM((nz, 8, WIDE), F32),
            pltpu.VMEM((8, WIDE), F32),
            dma((2,)),
            dma((parts, COPIES)),
            dma((parts, COPIES)),
            dma((parts, SPAN)),
            dma((parts, SPAN)),
            dma((parts, 3)),
            dma((parts, 3)),
            dma((ny, X_HI)),
            dma((ny, X_HI)),
            dma((X_HI, ny)),
            dma((nx, ny)),
            dma((X_HI,)),
            dma((nx,)),
            dma((ny,)),
            dma((ny,)),
            dma((nz,)),
            dma((nz,)),
            dma,
            dma,
            dma((4, nz)),
            dma((4, nz)),
        ],
        compiler_params=pltpu.CompilerParams(
            collective_id=0, has_side_effects=True, vmem_limit_bytes=60 * 2**20
        ),
        name="attention_block",
    )(x, norm_gain, cot, w_qkv, w_out)
    outs = hand_over(block_out, frames_grad, qkv_share, out_share, gain_sum)
    return (
        outs[0].reshape(frames.shape),
        outs[1].reshape(frames.shape),
        outs[2],
        outs[3],
        outs[4],
    )


def solution(mesh):
    in_specs = (P(("tm", "inner"), None, None), P(), P(), P(), P(("tm", "inner"), None, None))
    out_specs = (
        P(("tm", "inner"), None, None),
        P(("tm", "inner"), None, None),
        P("inner", "tm"),
        P("inner", "tm"),
        P("inner"),
    )
    return jax.shard_map(shards, mesh=mesh, in_specs=in_specs, out_specs=out_specs, check_vma=False)
```

```python
import functools
import math

import jax
import jax.numpy as jnp
from jax import lax
from jax.experimental import pallas as pl
from jax.experimental.pallas import tpu as pltpu
from jax.sharding import PartitionSpec as P

HEAD_DIM = 64
WINDOW = 4
CLIP_MAX = 256
EPSILON = 1e-06
SPAN = 2 * WINDOW + 1
WIDE = 128
ROWS = 64
COPIES = 21
CORES = 2
X_LO = 2
X_HI = 2
MESH = pl.DeviceIdType.MESH
F32 = jnp.float32
BF16 = jnp.bfloat16


def dot(a, b, dims=((1,), (0,))):
    return lax.dot_general(a, b, (dims, ((), ())), preferred_element_type=F32)


def split(wide_vals):
    high = wide_vals.astype(BF16)
    low = (wide_vals - high.astype(F32)).astype(BF16)
    return jnp.concatenate([high, low], axis=1)


def remote(source, target, ssem, rsem, where):
    return pltpu.make_async_remote_copy(
        src_ref=source,
        dst_ref=target,
        send_sem=ssem,
        recv_sem=rsem,
        device_id=where,
        device_id_type=MESH,
    )


def turned(value, step, count):
    return lax.rem(value + step, count)


def block_kernel(
    sizes,
    x_ref,
    gain_ref,
    cot_ref,
    wqkv_hbm,
    wout_hbm,
    bo_ref,
    fg_ref,
    wq_ref,
    wo_ref,
    gout_ref,
    wqkv_ref,
    wout_ref,
    xn,
    halo,
    comp,
    rcomp,
    wd,
    stack,
    dqkv_ref,
    unit,
    spread,
    ones,
    pick,
    spill,
    right_own,
    right_other,
    nleft_own,
    nleft_other,
    mleft_own,
    mleft_other,
    left_t,
    total,
    f0_send,
    f0_recv,
    f1_send,
    f1_recv,
    n_total,
    n0_send,
    n0_recv,
    n1_send,
    n1_recv,
    z_total,
    z_send,
    z_recv,
    final_send,
    final_recv,
    gain_core,
    gain_y,
    gain_x,
    gain_z,
    gain_last,
    load_sem,
    send_sem,
    recv_sem,
    csend_sem,
    crecv_sem,
    gsend_sem,
    grecv_sem,
    f0_ssem,
    f0_rsem,
    f1_ssem,
    f1_rsem,
    n0_ssem,
    n0_rsem,
    n1_ssem,
    n1_rsem,
    z_ssem,
    z_rsem,
    final_ssem,
    final_rsem,
    gain_ssem,
    gain_rsem,
):
    tm_size, inner, clip, inv_root = sizes
    frames_all = tm_size * inner
    tokens, width = x_ref.shape
    pairs = width // WIDE
    parts = tokens // ROWS
    ny, nx = tm_size // X_HI, X_HI * X_LO
    nz = inner // (X_LO * CORES)
    half_width = width // CORES
    share = 3 * width // tm_size
    block = 4 * width // tm_size
    side_rows = half_width // 2
    z_rows = half_width // nz
    final_rows = z_rows // CORES

    tm_at = lax.axis_index("tm")
    inner_at = lax.axis_index("inner")
    f = tm_at * inner + inner_at
    odd = lax.rem(f, 2)
    core = lax.rem(inner_at, CORES)
    z = lax.rem(lax.div(inner_at, CORES), nz)
    x_lo = lax.div(inner_at, CORES * nz)
    x_hi = lax.rem(tm_at, X_HI)
    x = x_hi * X_LO + x_lo
    y = lax.div(tm_at, X_HI)
    active = x_lo == core

    def at(offset):
        g = lax.rem(f + offset + frames_all, frames_all)
        return (lax.div(g, inner), lax.rem(g, inner))

    def device(yy, xx, zz, cc):
        return (
            yy * X_HI + lax.div(xx, X_LO),
            (lax.rem(xx, X_LO) * nz + zz) * CORES + cc,
        )

    partner = device(y, x, z, 1 - core)
    others = [j for j in range(-WINDOW, WINDOW + 1) if j != 0]
    peers = [at(j) for j in others]
    peers += [device(turned(y, d, ny), x, z, core) for d in range(1, ny)]
    peers += [device(y, turned(x, d, nx), z, core) for d in range(1, nx)]
    peers += [device(y, x, turned(z, d, nz), core) for d in range(1, nz)]
    barrier = pltpu.get_barrier_semaphore()
    for peer in peers:
        pl.semaphore_signal(barrier, inc=1, device_id=peer, device_id_type=MESH)

    load_qkv = pltpu.make_async_copy(wqkv_hbm, wqkv_ref, load_sem.at[0])
    load_out = pltpu.make_async_copy(wout_hbm, wout_ref, load_sem.at[1])
    load_qkv.start()
    load_out.start()

    def normalize(p):
        rows = slice(p * ROWS, (p + 1) * ROWS)
        wide_vals = x_ref[rows, :].astype(F32)
        center = wide_vals - jnp.mean(wide_vals, axis=-1, keepdims=True)
        variance = jnp.mean(center * center, axis=-1, keepdims=True)
        spread_one = lax.rsqrt(variance + EPSILON)
        unit_rows = center * spread_one
        unit[rows, :] = unit_rows
        spread[rows, :] = spread_one
        normed = (unit_rows * gain_ref[...].reshape(1, width)).astype(BF16)
        xn[2, p, :, 0:width] = normed
        xn[2, p, :, width : 2 * width] = cot_ref[rows, :]
        for i in range(CORES):
            nleft_own[i, rows, :] = normed[:, i * half_width : (i + 1) * half_width]

    normalize(0)

    def columns(c, part, size=WIDE):
        return pl.ds(pl.multiple_of(part * width + c * size, size), size)

    def copy(p, k):
        if k < 8:
            way = k // 2
            rows = pl.ds(k % 2 * (ROWS // 2), ROWS // 2)
            source = xn.at[(2, 2, 1, 3)[way], p, rows]
            target = xn.at[(1, 3, 0, 4)[way], p, rows]
            where = at((2, -2, 2, -2)[way])
        elif k == 8:
            source = halo.at[p, 4]
            target = halo.at[p, 3 + 2 * odd]
            where = partner
        else:
            slot = (2, 6, 8 - 8 * odd)[(k - 9) % 3]
            part = (k - 9) // 3
            lanes = pl.ds(part * width, width)
            source = halo.at[p, slot, :, lanes]
            target = halo.at[p, slot - 1 + 2 * odd, :, lanes]
            where = partner
        return remote(source, target, send_sem.at[p, k], recv_sem.at[p, k], where)

    def comp_copy(p, j):
        k = j + WINDOW
        return remote(
            comp.at[p, k],
            rcomp.at[p, SPAN - 1 - k],
            csend_sem.at[p, k],
            crecv_sem.at[p, k],
            at(j),
        )

    normed_copy = remote(
        nleft_own.at[1 - core], nleft_other, gsend_sem.at[0, 2], grecv_sem.at[0, 2], partner
    )

    def left_copy(p):
        return remote(
            mleft_own.at[1 - core, p],
            mleft_other.at[p],
            gsend_sem.at[p, 0],
            grecv_sem.at[p, 0],
            partner,
        )

    def right_copy(p):
        return remote(
            right_own.at[p], right_other.at[p], gsend_sem.at[p, 1], grecv_sem.at[p, 1], partner
        )

    pl.semaphore_wait(barrier, len(peers))

    def start_own(p):
        for k in (0, 2, 1, 3):
            copy(p, k).start()

    def relay_half(p, half):
        for way in range(2):
            copy(p, 2 * way + half).wait_recv()
            copy(p, 4 + 2 * way + half).start()

    def relay(p):
        relay_half(p, 0)
        relay_half(p, 1)

    start_own(0)
    for p in range(1, parts):
        normalize(p)
    normed_copy.start()

    row_at = lax.broadcasted_iota(jnp.int32, (2 * WIDE, WIDE), 0)
    lane_at = lax.broadcasted_iota(jnp.int32, (2 * WIDE, WIDE), 1)
    same = (lax.rem(row_at, WIDE) // HEAD_DIM) == (lane_at // HEAD_DIM)
    ones[...] = jnp.where(same, HEAD_DIM**-0.5, 0.0).astype(BF16)
    row_at = lax.broadcasted_iota(jnp.int32, pick.shape, 0)
    lane_at = lax.broadcasted_iota(jnp.int32, pick.shape, 1)
    pick[...] = jnp.where(row_at == lane_at * HEAD_DIM, 1.0, 0.0).astype(BF16)
    row_at = lax.broadcasted_iota(jnp.int32, spill.shape, 0)
    lane_at = lax.broadcasted_iota(jnp.int32, spill.shape, 1)
    spill[...] = jnp.where(lane_at // HEAD_DIM == row_at, 1.0, 0.0).astype(BF16)

    def place(p, value, start, stride, lead):
        left = value.shape[1]
        taken = 0
        while taken < left:
            t = (start + taken) // stride
            into = start + taken - t * stride
            count = min(left - taken, stride - into)
            right_own[p, t, :, lead + into : lead + into + count] = value[:, taken : taken + count]
            taken += count

    relay_half(0, 0)
    start_own(1)
    load_qkv.wait()
    load_out.wait()

    def project(rows_in, put):
        for part in range(3):
            weight = wqkv_ref[:, part * width : (part + 1) * width]
            put(part, dot(rows_in[:, 0:width], weight).astype(BF16))
        put(3, dot(rows_in[:, width : 2 * width], wout_ref[...], ((1,), (1,))).astype(BF16))

    def put_own(part, value):
        for p in range(parts):
            halo[p, 4, :, part * width : (part + 1) * width] = value[p * ROWS : (p + 1) * ROWS]

    project(xn[2].reshape(tokens, 2 * width), put_own)

    copy(0, 8).start()

    def project_others(p):
        for k in range(4, 8):
            copy(p, k).wait_recv()

        @pl.when(p + 1 < parts)
        def _():
            copy(p + 1, 8).start()

        rows_in = jnp.concatenate([xn[1, p], xn[3, p], xn[0, p], xn[4, p]], axis=0)

        def put(part, value):
            for i, k in enumerate((2, 6, 0, 8)):
                halo[p, k, :, part * width : (part + 1) * width] = value[
                    i * ROWS : (i + 1) * ROWS
                ]

            for i in range(3):
                copy(p, 9 + 3 * part + i).start()

        project(rows_in, put)

    def attend(p):
        for k in range(8, COPIES):
            copy(p, k).wait_recv()
        rows = pl.ds(pl.multiple_of(p * ROWS, ROWS), ROWS)

        @pl.loop(0, pairs, unroll=pairs)
        def _(c):
            def load(k, part):
                return halo[p, k, :, columns(c, part)].astype(F32)

            query = load(4, 0)
            grad = halo[p, 4, :, columns(c, 3)]
            products = [split(query * load(k, 1)) for k in range(SPAN)]
            scores = dot(jnp.concatenate(products, axis=0), ones[...])
            products = [grad * halo[p, k, :, columns(c, 2)] for k in range(SPAN)]
            dots = dot(jnp.concatenate(products, axis=0), ones[0:WIDE])
            score = []
            for k in range(SPAN):
                g = f + (k - WINDOW)
                inside = (g >= 0) & (g < frames_all)
                inside = inside & (lax.div(g + clip, clip) == lax.div(f + clip, clip))
                cap = jnp.where(inside, 3e38, -1e30).astype(F32)
                score.append(jnp.minimum(scores[k * ROWS : (k + 1) * ROWS], cap))
            top = functools.reduce(jnp.maximum, score)
            raised = [jnp.exp(s - top) for s in score]
            scale = 1.0 / functools.reduce(jnp.add, raised)
            soft = [e * scale for e in raised]
            mixed = jnp.zeros((ROWS, WIDE), F32)
            centre = jnp.zeros((ROWS, WIDE), F32)
            weight_at = pl.ds(pl.multiple_of(c * 2 * WIDE, WIDE), WIDE)
            slope_at = pl.ds(pl.multiple_of(c * 2 * WIDE + WIDE, WIDE), WIDE)
            for k in range(SPAN):
                weight = soft[k].astype(BF16)
                wd[k, :, weight_at] = weight
                mixed += weight.astype(F32) * load(k, 2)
                centre += soft[k] * dots[k * ROWS : (k + 1) * ROWS]
            side = lax.div(c, pairs // CORES)
            mleft_own[side, p, :, columns(lax.rem(c, pairs // CORES), 0)] = mixed.astype(BF16)
            query_grad = jnp.zeros((ROWS, WIDE), F32)
            for k in range(SPAN):
                gap = dots[k * ROWS : (k + 1) * ROWS] - centre
                slope = (soft[k] * gap).astype(BF16)
                wd[k, :, slope_at] = slope
                query_grad += slope.astype(F32) * load(k, 1)
            dqkv_ref[rows, columns(c, 0)] = query_grad.astype(BF16)

        small = dot(wd[...].reshape(SPAN * ROWS, 2 * width), pick[...])
        for k in range(SPAN):
            packed = small[k * ROWS : k * ROWS + 16]
            for r in range(1, ROWS // 16):
                at_row = k * ROWS + r * 16
                packed += pltpu.roll(small[at_row : at_row + 16], 32 * r, 1)
            if k == WINDOW:
                rcomp[p, k] = packed.astype(BF16)
            else:
                comp[p, k] = packed.astype(BF16)
                comp_copy(p, k - WINDOW).start()

    def collect(p):
        for j in others:
            comp_copy(p, j).wait_recv()
        rows = pl.ds(pl.multiple_of(p * ROWS, ROWS), ROWS)
        for k in range(SPAN):
            packed = rcomp[p, k].astype(F32)
            for r in range(ROWS // 16):
                value = packed if r == 0 else pltpu.roll(packed, WIDE - 32 * r, 1)
                stack[k * ROWS + r * 16 : k * ROWS + (r + 1) * 16, :] = value.astype(BF16)

        @pl.loop(0, pairs, unroll=pairs)
        def _(c):
            wide = dot(stack[...], spill[:, columns(c, 0, 2 * WIDE)])
            key_grad = jnp.zeros((ROWS, WIDE), F32)
            value_grad = jnp.zeros((ROWS, WIDE), F32)
            for k in range(SPAN):
                piece = wide[k * ROWS : (k + 1) * ROWS]
                value_grad += piece[:, :WIDE] * halo[p, k, :, columns(c, 3)].astype(F32)
                key_grad += piece[:, WIDE:] * halo[p, k, :, columns(c, 0)].astype(F32)
            dqkv_ref[rows, columns(c, 1)] = key_grad.astype(BF16)
            dqkv_ref[rows, columns(c, 2)] = value_grad.astype(BF16)

        for m in range(3 * pairs):
            value = dqkv_ref[rows, m * WIDE : (m + 1) * WIDE]
            place(p, value, m * WIDE, share, 0)
        left_copy(p).start()
        right_copy(p).start()

    relay_half(0, 1)
    start_own(2)
    for p in range(parts):
        for m in range(pairs):
            value = cot_ref[p * ROWS : (p + 1) * ROWS, m * WIDE : (m + 1) * WIDE]
            place(p, value, m * WIDE, width // tm_size, share)

    normed_copy.wait_recv()
    left_t[0, :, 0:tokens] = nleft_own[core].T
    left_t[0, :, tokens : 2 * tokens] = nleft_other[...].T

    relay(1)
    start_own(3)
    project_others(0)

    @pl.loop(0, parts)
    def _(p):
        @pl.when((p > 0) & (p + 2 < parts))
        def _():
            relay(p + 2)

        @pl.when((p > 0) & (p + 3 < parts))
        def _():
            start_own(p + 3)

        attend(p)

        @pl.when(p == 0)
        def _():
            relay(2)

        @pl.when(p + 1 < parts)
        def _():
            project_others(p + 1)

        @pl.when(p > 0)
        def _():
            collect(p - 1)

    collect(parts - 1)

    def f0_copy(yy, xh):
        return remote(
            f0_send.at[yy, xh],
            f0_recv.at[y, xh],
            f0_ssem.at[yy, xh],
            f0_rsem.at[y, xh],
            device(yy, x, z, core),
        )

    def f1_copy(yy, xh):
        return remote(
            f1_send.at[xh, yy],
            f1_recv.at[x, yy],
            f1_ssem.at[xh, yy],
            f1_rsem.at[x, yy],
            device(y, xh * X_LO + core, z, core),
        )

    left_t[1, :, 0:tokens] = mleft_own[core].reshape(tokens, half_width).T
    for p in range(parts):
        left_copy(p).wait_recv()
    left_t[1, :, tokens : 2 * tokens] = mleft_other[...].reshape(tokens, half_width).T
    for p in range(parts):
        right_copy(p).wait_recv()

    @pl.loop(0, tm_size, unroll=2)
    def _(i):
        t = turned(i + X_HI, y * X_HI, tm_size)
        yy, xh = lax.div(t, X_HI), lax.rem(t, X_HI)
        right = jnp.concatenate(
            [right_own[p, t] for p in range(parts)] + [right_other[p, t] for p in range(parts)],
            axis=0,
        )
        first = dot(left_t[0], right)
        last = (block - 1) // WIDE * WIDE
        second = dot(left_t[1], right[:, last:])
        lane = lax.broadcasted_iota(jnp.int32, second.shape, 1)
        tail = jnp.where(lane < share - last, first[:, last:], second)
        total[t, :, 0:last] = first[:, :last]
        total[t, :, last:block] = tail
        f0_send[yy, xh, :, 0:last] = first[:side_rows, :last].astype(BF16)
        f0_send[yy, xh, :, last:block] = tail[:side_rows].astype(BF16)
        f1_send[xh, yy, :, 0:last] = first[side_rows:, :last].astype(BF16)
        f1_send[xh, yy, :, last:block] = tail[side_rows:].astype(BF16)

        @pl.when(yy != y)
        def _():
            f0_copy(yy, xh).start()

        @pl.when(xh * X_LO + core != x)
        def _():
            f1_copy(yy, xh).start()

    normed_grad = dot(dqkv_ref[...], wqkv_ref[...], ((1,), (1,)))
    unit_rows = unit[...]
    gain_part = jnp.sum(normed_grad * unit_rows, axis=0, keepdims=True)
    gain_core[core] = jnp.zeros((8, WIDE), F32)
    for i in range(pairs):
        gain_core[core, i : i + 1, :] = gain_part[:, i * WIDE : (i + 1) * WIDE]

    def gain_exchange(buffer, own, count, spot, slot):
        return [
            remote(
                buffer.at[own],
                buffer.at[own],
                gain_ssem.at[slot, d],
                gain_rsem.at[slot, d],
                spot(turned(own, d, count)),
            )
            for d in range(1, count)
        ]

    def gain_sum(buffer, count):
        return functools.reduce(jnp.add, [buffer[i] for i in range(count)])

    core_gain = gain_exchange(gain_core, core, CORES, lambda cc: device(y, x, z, cc), 0)
    y_gain = gain_exchange(gain_y, y, ny, lambda yy: device(yy, x, z, core), 1)
    x_gain = gain_exchange(gain_x, x, nx, lambda xx: device(y, xx, z, core), 2)
    z_gain = gain_exchange(gain_z, z, nz, lambda zz: device(y, x, zz, core), 3)
    for move in core_gain:
        move.start()

    scaled = normed_grad * gain_ref[...].reshape(1, width)
    mean_one = jnp.mean(scaled, axis=-1, keepdims=True)
    second = jnp.mean(scaled * unit_rows, axis=-1, keepdims=True)
    back = spread[...] * (scaled - mean_one - unit_rows * second)
    fg_ref[...] = (cot_ref[...].astype(F32) + back).astype(BF16)
    mixed_out = x_ref[...].astype(F32)
    for i in range(CORES):
        mixed_half = mleft_own[i].reshape(tokens, half_width)
        mixed_out += dot(mixed_half, wout_ref[i * half_width : (i + 1) * half_width, :])
    bo_ref[...] = mixed_out.astype(BF16)

    for move in core_gain:
        move.wait_recv()
    gain_y[y] = gain_sum(gain_core, CORES)
    for move in y_gain:
        move.start()

    def n0_copy(xh):
        return remote(
            n0_send.at[xh],
            n0_recv.at[x],
            n0_ssem.at[xh],
            n0_rsem.at[x],
            device(y, xh * X_LO + core, z, core),
        )

    def n1_copy(yy):
        return remote(
            n1_send.at[yy],
            n1_recv.at[y],
            n1_ssem.at[yy],
            n1_rsem.at[y],
            device(yy, x, z, core),
        )

    def z_copy(zz):
        return remote(
            z_send.at[zz], z_recv.at[z], z_ssem.at[zz], z_rsem.at[z], device(y, x, zz, core)
        )

    def arrived(buffer, spot, sem):
        remote(buffer.at[spot], buffer.at[spot], sem.at[spot], sem.at[spot], partner).wait_recv()
        return buffer[spot].astype(F32)

    for step in range(1, X_HI + 1):
        xh = turned(x_hi, step, X_HI)
        value = total[y * X_HI + xh, 0:side_rows, :]
        for d in range(1, ny):
            value = value + arrived(f0_recv, (turned(y, d, ny), xh), f0_rsem)
        goal = xh * X_LO + core

        @pl.when(goal != x)
        def _():
            n0_send[xh] = value.astype(BF16)
            n0_copy(xh).start()

        @pl.when(goal == x)
        def _():
            n_total[0] = value

    @pl.when(active)
    def _():
        for step in range(1, ny + 1):
            yy = turned(y, step, ny)
            value = total[yy * X_HI + x_hi, side_rows : 2 * side_rows, :]
            for d in range(1, nx):
                value = value + arrived(f1_recv, (turned(x, d, nx), yy), f1_rsem)
            if step < ny:
                n1_send[yy] = value.astype(BF16)
                n1_copy(yy).start()
            else:
                n_total[1] = value

    for move in y_gain:
        move.wait_recv()
    gain_x[x] = gain_sum(gain_y, ny)
    for move in x_gain:
        move.start()

    @pl.when(active)
    def _():
        for side in range(2):
            value = n_total[side]
            for d in range(1, nx if side == 0 else ny):
                if side == 0:
                    value = value + arrived(n0_recv, turned(x, d, nx), n0_rsem)
                else:
                    value = value + arrived(n1_recv, turned(y, d, ny), n1_rsem)
            for i in range(nz // 2):
                zz = side * (nz // 2) + i
                piece = value[i * z_rows : (i + 1) * z_rows]
                z_total[zz] = piece
                z_send[zz] = piece.astype(BF16)

                @pl.when(zz != z)
                def _():
                    z_copy(zz).start()

    for move in x_gain:
        move.wait_recv()
    gain_z[z] = gain_sum(gain_x, nx)
    for move in z_gain:
        move.start()

    final = remote(final_send, final_recv, final_ssem, final_rsem, partner)

    def deliver(value):
        last = share // WIDE * WIDE
        wq_ref[:, 0:last] = value[:, :last]
        tail = value[:, last : last + WIDE]
        wq_ref[:, last:share] = tail[:, : share - last]
        if share == last:
            wo_ref[...] = tail
        else:
            count = block - share
            wo_ref[...] = pltpu.roll(tail, WIDE - (share - last), 1)[:, :count]

    @pl.when(active)
    def _():
        value = z_total[z]
        for d in range(1, nz):
            value = value + arrived(z_recv, turned(z, d, nz), z_rsem)
        value = value * inv_root
        lower = value[:final_rows]
        upper = value[final_rows:]
        final_send[...] = jnp.where(core == 0, upper, lower)
        final.start()
        deliver(jnp.where(core == 0, lower, upper))

    @pl.when(jnp.logical_not(active))
    def _():
        final.wait_recv()
        deliver(final_recv[...])

    for move in z_gain:
        move.wait_recv()
    gain_last[...] = gain_sum(gain_z, nz) * inv_root
    cut = width // inner
    row_one = lax.div(inner_at * cut, WIDE)
    lead = lax.rem(inner_at * cut, WIDE)
    low = jnp.broadcast_to(gain_last[pl.ds(row_one, 1), :], (8, WIDE))
    high = jnp.broadcast_to(gain_last[pl.ds(row_one + 1, 1), :], (8, WIDE))
    lane = lax.broadcasted_iota(jnp.int32, (8, WIDE), 1)
    shift = lax.rem(WIDE - lead, WIDE)
    merged = jnp.where(
        lane < WIDE - lead, pltpu.roll(low, shift, 1), pltpu.roll(high, shift, 1)
    )
    gout_ref[...] = merged[0:1, :cut]

    normed_copy.wait_send()
    for move in core_gain + y_gain + x_gain + z_gain:
        move.wait_send()

    @pl.loop(0, parts)
    def _(p):
        for k in range(COPIES):
            copy(p, k).wait_send()
        for j in others:
            comp_copy(p, j).wait_send()
        left_copy(p).wait_send()
        right_copy(p).wait_send()

    for xh in range(X_HI):
        for yy in range(ny):

            @pl.when(yy != y)
            def _():
                f0_copy(yy, xh).wait_send()

            @pl.when(xh * X_LO + core != x)
            def _():
                f1_copy(yy, xh).wait_send()

        @pl.when(xh * X_LO + core != x)
        def _():
            n0_copy(xh).wait_send()

    @pl.when(active)
    def _():
        for yy in range(ny):

            @pl.when(yy != y)
            def _():
                n1_copy(yy).wait_send()

        for zz in range(nz):

            @pl.when(zz != z)
            def _():
                z_copy(zz).wait_send()

        final.wait_send()


def copy_kernel(*refs):
    count = len(refs) // 2
    for source, target in zip(refs[:count], refs[count:], strict=True):
        target[...] = source[...].reshape(target.shape)


def hand_over(*arrays):
    vmem = pl.BlockSpec(memory_space=pltpu.VMEM)
    shapes = [a.shape for a in arrays[:-1]] + [(arrays[-1].size,)]
    return pl.pallas_call(
        copy_kernel,
        out_shape=tuple(
            jax.ShapeDtypeStruct(shape, a.dtype) for shape, a in zip(shapes, arrays, strict=True)
        ),
        in_specs=[vmem] * len(arrays),
        out_specs=(vmem,) * len(arrays),
        name="hand_over",
    )(*arrays)


def shards(frames, norm_gain, w_qkv, w_out, cotangent):
    tm_size, inner = lax.axis_size("tm"), lax.axis_size("inner")
    width = frames.shape[-1]
    tokens = frames.shape[0] * frames.shape[1]
    frames_all = tm_size * inner
    x = frames.reshape(tokens, width)
    cot = cotangent.reshape(tokens, width)
    ny, nx = tm_size // X_HI, X_HI * X_LO
    nz = inner // (X_LO * CORES)
    parts = tokens // ROWS
    half = width // CORES
    share = 3 * width // tm_size
    block = 4 * width // tm_size
    side = half // 2
    z_rows = half // nz
    final_rows = z_rows // CORES
    inv_root = 1.0 / math.sqrt(tokens * frames_all)
    sizes = (tm_size, inner, min(CLIP_MAX, frames_all), inv_root)
    vmem = pl.BlockSpec(memory_space=pltpu.VMEM)
    hbm = pl.BlockSpec(memory_space=pl.ANY)
    dma = pltpu.SemaphoreType.DMA
    block_out, frames_grad, qkv_share, out_share, gain_sum = pl.pallas_call(
        functools.partial(block_kernel, sizes),
        out_shape=(
            jax.ShapeDtypeStruct((tokens, width), BF16),
            jax.ShapeDtypeStruct((tokens, width), BF16),
            jax.ShapeDtypeStruct((final_rows, share), F32),
            jax.ShapeDtypeStruct((final_rows, block - share), F32),
            jax.ShapeDtypeStruct((1, width // inner), F32),
        ),
        in_specs=[vmem, vmem, vmem, hbm, hbm],
        out_specs=(vmem,) * 5,
        scratch_shapes=[
            pltpu.VMEM(w_qkv.shape, BF16),
            pltpu.VMEM(w_out.shape, BF16),
            pltpu.VMEM((5, parts, ROWS, 2 * width), BF16),
            pltpu.VMEM((parts, SPAN, ROWS, 4 * width), BF16),
            pltpu.VMEM((parts, SPAN, 16, WIDE), BF16),
            pltpu.VMEM((parts, SPAN, 16, WIDE), BF16),
            pltpu.VMEM((SPAN, ROWS, 2 * width), BF16),
            pltpu.VMEM((SPAN * ROWS, WIDE), BF16),
            pltpu.VMEM((tokens, 3 * width), BF16),
            pltpu.VMEM((tokens, width), F32),
            pltpu.VMEM((tokens, 1), F32),
            pltpu.VMEM((2 * WIDE, WIDE), BF16),
            pltpu.VMEM((2 * width, WIDE), BF16),
            pltpu.VMEM((WIDE, 2 * width), BF16),
            pltpu.VMEM((parts, tm_size, ROWS, block), BF16),
            pltpu.VMEM((parts, tm_size, ROWS, block), BF16),
            pltpu.VMEM((CORES, tokens, half), BF16),
            pltpu.VMEM((tokens, half), BF16),
            pltpu.VMEM((CORES, parts, ROWS, half), BF16),
            pltpu.VMEM((parts, ROWS, half), BF16),
            pltpu.VMEM((2, half, 2 * tokens), BF16),
            pltpu.VMEM((tm_size, half, block), F32),
            pltpu.VMEM((ny, X_HI, side, block), BF16),
            pltpu.VMEM((ny, X_HI, side, block), BF16),
            pltpu.VMEM((X_HI, ny, side, block), BF16),
            pltpu.VMEM((nx, ny, side, block), BF16),
            pltpu.VMEM((2, side, block), F32),
            pltpu.VMEM((X_HI, side, block), BF16),
            pltpu.VMEM((nx, side, block), BF16),
            pltpu.VMEM((ny, side, block), BF16),
            pltpu.VMEM((ny, side, block), BF16),
            pltpu.VMEM((nz, z_rows, block), F32),
            pltpu.VMEM((nz, z_rows, block), BF16),
            pltpu.VMEM((nz, z_rows, block), BF16),
            pltpu.VMEM((final_rows, block), F32),
            pltpu.VMEM((final_rows, block), F32),
            pltpu.VMEM((CORES, 8, WIDE), F32),
            pltpu.VMEM((ny, 8, WIDE), F32),
            pltpu.VMEM((nx, 8, WIDE), F32),
            pltpu.VMEM((nz, 8, WIDE), F32),
            pltpu.VMEM((8, WIDE), F32),
            dma((2,)),
            dma((parts, COPIES)),
            dma((parts, COPIES)),
            dma((parts, SPAN)),
            dma((parts, SPAN)),
            dma((parts, 3)),
            dma((parts, 3)),
            dma((ny, X_HI)),
            dma((ny, X_HI)),
            dma((X_HI, ny)),
            dma((nx, ny)),
            dma((X_HI,)),
            dma((nx,)),
            dma((ny,)),
            dma((ny,)),
            dma((nz,)),
            dma((nz,)),
            dma,
            dma,
            dma((4, nz)),
            dma((4, nz)),
        ],
        compiler_params=pltpu.CompilerParams(
            collective_id=0, has_side_effects=True, vmem_limit_bytes=60 * 2**20
        ),
        name="attention_block",
    )(x, norm_gain, cot, w_qkv, w_out)
    outs = hand_over(block_out, frames_grad, qkv_share, out_share, gain_sum)
    return (
        outs[0].reshape(frames.shape),
        outs[1].reshape(frames.shape),
        outs[2],
        outs[3],
        outs[4],
    )


def solution(mesh):
    in_specs = (P(("tm", "inner"), None, None), P(), P(), P(), P(("tm", "inner"), None, None))
    out_specs = (
        P(("tm", "inner"), None, None),
        P(("tm", "inner"), None, None),
        P("inner", "tm"),
        P("inner", "tm"),
        P("inner"),
    )
    return jax.shard_map(shards, mesh=mesh, in_specs=in_specs, out_specs=out_specs, check_vma=False)
```
